32 devices in a mesh: dp: 8 (over z, y), seq: 4 (over x, core).
Axes of the slice: x: 2, y: 2, z: 4, core: 2. Of those that a mesh axis runs over, the one named last changes fastest.
Arguments:
- tokens: bfloat16 [16, 1024, 768], P('dp', 'seq'), may hold values from -6 to 6
- lengths: int32 [16, 4], P('dp'), may hold values from 0 to 1024, as said below
- out_grad: bfloat16 [16, 1024, 768], P('dp', 'seq'), may hold values from -6 to 6
- mats: float32 [768, 9216], P(None, ('dp', 'seq'))
- vectors: float32 [9216], P(('dp', 'seq'))
- moment_mats: float32 [768, 9216], P(None, ('dp', 'seq')), may hold values from -40 to 40
- second_mats: float32 [768, 9216], P(None, ('dp', 'seq')), may hold values from 4.096 to 16.384
- moment_vecs: float32 [9216], P(('dp', 'seq')), may hold values from -80 to 80
- second_vecs: float32 [9216], P(('dp', 'seq')), may hold values from 16.384 to 65.536
Outputs:
- block_out: bfloat16 [16, 1024, 768], P('dp', 'seq')
- input_grad: float32 [16, 1024, 768], P('dp', 'seq')
- new_mats: float32 [768, 9216], P(None, ('dp', 'seq'))
- new_moment_mats: float32 [768, 9216], P(None, ('dp', 'seq'))
- new_second_mats: float32 [768, 9216], P(None, ('dp', 'seq'))
- new_vectors: float32 [9216], P(('dp', 'seq'))
- new_moment_vecs: float32 [9216], P(('dp', 'seq'))
- new_second_vecs: float32 [9216], P(('dp', 'seq'))
The draws below stay inside these ranges and needn't reach their ends.
Inputs may be any that keep to these rules, and one draw needn't show every extreme that they name: Each row holds the lengths of the documents packed into one sequence, in order, summing to 1024; empty documents occur. In every block of 2 rows (the sequences of one index of dp) one row, drawn from the seed, is a single document of 1024 tokens.
All inputs are finite; a program needn't handle non-finite values.
Results may differ from the reference program's by a relative error of at most 0.018.
Values may be sent and summed in bfloat16 or wider, within the bound.
No kernel may reach another device: no remote copies, remote signals or barrier semaphores. Data moves between devices by JAX's collectives and lax.ppermute only.
A program may use at most 192 MiB of HBM per device.

```python
import math
import jax
import jax.numpy as jnp
from jax import lax

D = 768
HEADS = 12
HEAD_DIM = 64
FF = 3072
SEQS = 2
LENGTH = 1024
NDOC = 4
STEP = 10
BATCH = 16
COLS = 9216
VEC = 9216
N_DP = 8


def draw_mats(key, part):
    key = jax.random.fold_in(key, 11)
    column = jnp.arange(4 * D + 2 * FF)
    base_scale = D ** (-0.5)
    column_scale = jnp.where(column < 3 * D, base_scale, jnp.where(column < 4 * D, 8.0 * base_scale, jnp.where(column < 4 * D + FF, base_scale, 2.0 * FF ** (-0.5))))
    values = jax.random.normal(key, (D, 4 * D + 2 * FF), jnp.float32)
    return values * column_scale[None, :].astype(jnp.float32)


def draw_vectors(key, part):
    key = jax.random.fold_in(key, 12)
    entries = 8 * D + FF
    position = jnp.arange(entries)
    gain_slot = (position >= 3 * D) & (position < 4 * D) | (position >= 5 * D) & (position < 6 * D)
    noise = jax.random.normal(key, (entries,), jnp.float32)
    return jnp.where(gain_slot, 1.0 + 0.15 * noise, 0.3 * noise).astype(jnp.float32)


def draw_lengths(key, part):
    key = jax.random.fold_in(key, 13)
    cut_key, pick_key = jax.random.split(key)
    row_total = SEQS * N_DP
    cuts = jax.random.randint(cut_key, (row_total, NDOC - 1), 0, LENGTH + 1)
    cuts = jnp.sort(cuts, axis=-1)
    edges = jnp.concatenate([jnp.zeros((row_total, 1), jnp.int32), cuts.astype(jnp.int32), jnp.full((row_total, 1), LENGTH, jnp.int32)], axis=-1)
    doc_sizes = edges[:, 1:] - edges[:, :-1]
    chosen = jax.random.randint(pick_key, (N_DP,), 0, SEQS)
    row_ids = jnp.arange(row_total)
    whole_row = row_ids % SEQS == jnp.repeat(chosen, SEQS)
    single = jnp.concatenate([jnp.full((1,), LENGTH, jnp.int32), jnp.zeros((NDOC - 1,), jnp.int32)])
    return jnp.where(whole_row[:, None], single[None, :], doc_sizes).astype(jnp.int32)


def level_of(stream_key, extent, cuts, least, high):
    def one(dim, blocks):
        draws = jax.random.uniform(jax.random.fold_in(jax.random.fold_in(stream_key, 6), dim), (blocks,), jnp.float32, least / len(cuts), high / len(cuts))
        return jnp.repeat(jnp.exp(draws), extent[dim] // blocks).reshape((-1,) + (1,) * (len(extent) - dim - 1))

    loudness = one(*cuts[0])
    for cut in cuts[1:]:
        loudness = loudness * one(*cut)
    return loudness


def gaussian(stream_key, shape, deviation, reach, cuts=(), kind=jnp.bfloat16):
    level = level_of(stream_key, shape, cuts, -0.22, 0.18) if cuts else 1.0
    values = jax.random.normal(stream_key, shape, jnp.float32) * deviation * level
    return jnp.minimum(jnp.maximum(values, -reach), reach).astype(kind)


def setup_inputs(seed: int = 0) -> dict:
    splits = jax.random.split(jax.random.key(seed), 10)
    return {
        "tokens": gaussian(splits[0], (BATCH, LENGTH, D), 1.0, 6.0, ((0, 8), (1, 4))),
        "lengths": draw_lengths(jax.random.fold_in(splits[9], 71), 0),
        "out_grad": gaussian(splits[2], (BATCH, LENGTH, D), 1.0, 6.0, ((0, 8), (1, 4))),
        "mats": draw_mats(jax.random.fold_in(splits[9], 71), 0),
        "vectors": draw_vectors(jax.random.fold_in(splits[9], 71), 0),
        "moment_mats": gaussian(splits[5], (D, COLS), (0.055 * (SEQS * N_DP * LENGTH) ** 0.5), 40.0, ((1, 32),), jnp.float32),
        "second_mats": jnp.clip(jnp.exp(math.log(16.384) - 1.3862944 * jax.random.uniform(splits[6], (D, COLS), jnp.float32) ** level_of(splits[6], (D, COLS), ((1, 32),), -0.2, 0.2)), 4.096, 16.384),
        "moment_vecs": gaussian(splits[7], (VEC,), (0.11 * (SEQS * N_DP * LENGTH) ** 0.5), 80.0, ((0, 32),), jnp.float32),
        "second_vecs": jnp.clip(jnp.exp(math.log(65.536) - 1.3862944 * jax.random.uniform(splits[8], (VEC,), jnp.float32) ** level_of(splits[8], (VEC,), ((0, 32),), -0.2, 0.2)), 16.384, 65.536),
    }


@jax.custom_vjp
def low(v):
    return lax.optimization_barrier(v.astype(jnp.bfloat16)).astype(jnp.float32)

@jax.custom_vjp
def low_back(v):
    return v

def low_keep(v):
    return (low(v), None)

def low_pass(kept, grad):
    return (grad,)

def back_keep(v):
    return (v, None)

def back_low(kept, grad):
    return (low(grad),)
low.defvjp(low_keep, low_pass)
low_back.defvjp(back_keep, back_low)
norm_eps = 1e-05
first_decay = 0.9
second_decay = 0.999
adam_eps = 1e-08
rate_mats = 0.08
rate_vecs = 0.4
weight_decay = 0.01

def both_low(values):
    return low(low_back(values))

def matmul(left, right):
    return jnp.dot(left, right, precision=lax.Precision.HIGHEST)

def norm_apply(values, gain, shift):
    center = values - lax.optimization_barrier(jnp.mean(values, axis=-1, keepdims=True))
    spread = lax.optimization_barrier(jnp.mean(center * center, axis=-1, keepdims=True))
    return center * lax.rsqrt(spread + norm_eps) * gain + shift

def segments_of(lengths):
    ends = jnp.cumsum(lengths, axis=-1)
    positions = jnp.arange(LENGTH, dtype=jnp.int32)
    return lax.optimization_barrier(jnp.sum((positions[None, :, None] >= ends[:, None, :]).astype(jnp.int32), axis=-1))

def forward(inputs, mats, vectors, segment):
    weights = low(mats)
    biases = low(vectors)
    w_query = weights[:, 0:D]
    w_key = weights[:, D:2 * D]
    w_value = weights[:, 2 * D:3 * D]
    w_out = weights[:, 3 * D:4 * D]
    w_first = weights[:, 4 * D:4 * D + FF]
    w_second = weights[:, 4 * D + FF:]
    b_query = biases[0:D]
    b_value = biases[D:2 * D]
    b_out = biases[2 * D:3 * D]
    gain_one = biases[3 * D:4 * D]
    shift_one = biases[4 * D:5 * D]
    gain_two = biases[5 * D:6 * D]
    shift_two = biases[6 * D:7 * D]
    b_second = biases[7 * D:8 * D]
    b_first = biases[8 * D:]
    queries = both_low(matmul(inputs, w_query) + b_query)
    keys_all = both_low(matmul(inputs, w_key))
    values_all = both_low(matmul(inputs, w_value) + b_value)
    query_heads = queries.reshape(LENGTH, HEADS, HEAD_DIM)
    key_heads = keys_all.reshape(LENGTH, HEADS, HEAD_DIM)
    value_heads = values_all.reshape(LENGTH, HEADS, HEAD_DIM)
    scores = jnp.einsum('qhd,khd->hqk', query_heads, key_heads, precision=lax.Precision.HIGHEST) * HEAD_DIM ** (-0.5)
    same_doc = segment[:, None] == segment[None, :]
    scores = low_back(jnp.where(same_doc[None], scores, -1e+30))
    top_score = lax.optimization_barrier(jnp.max(scores, axis=-1, keepdims=True))
    exponent = jnp.exp(scores - top_score)
    attn_probs = low(exponent / lax.optimization_barrier(jnp.sum(exponent, axis=-1, keepdims=True)))
    attended = jnp.einsum('hqk,khd->qhd', attn_probs, value_heads, precision=lax.Precision.HIGHEST)
    attended = both_low(attended.reshape(LENGTH, D))
    branch = low_back(matmul(attended, w_out) + b_out)
    hidden = inputs + branch
    normed = norm_apply(hidden, gain_one, shift_one)
    inner = low_back(matmul(low(normed), w_first) + b_first)
    active = low(jax.nn.gelu(inner, approximate=False))
    feed = low_back(matmul(active, w_second.T) + b_second)
    return norm_apply(normed + feed, gain_two, shift_two)

def adamw(weight, gradient, moment, second, rate, decay):
    moment_new = first_decay * moment + (1.0 - first_decay) * gradient
    second_new = second_decay * second + (1.0 - second_decay) * gradient * gradient
    fixed_first = moment_new / (1.0 - first_decay ** STEP)
    fixed_second = second_new / (1.0 - second_decay ** STEP)
    weight_new = weight - rate * (fixed_first / (jnp.sqrt(fixed_second) + adam_eps) + decay * weight)
    return (weight_new, moment_new, second_new)

def reference(tokens, lengths, out_grad, mats, vectors, moment_mats, second_mats, moment_vecs, second_vecs):
    segments = segments_of(lengths)
    inputs_all = tokens.astype(jnp.float32)
    cotangents = out_grad.astype(jnp.float32)

    def one_sequence(carry, item):
        grad_mats, grad_vecs = carry
        inputs, cotangent, segment = item

        def run(values, weight_mats, weight_vecs):
            return forward(values, weight_mats, weight_vecs, segment)
        result, pull = jax.vjp(run, inputs, mats, vectors)
        d_inputs, d_mats, d_vecs = pull(cotangent)
        return ((grad_mats + d_mats, grad_vecs + d_vecs), (result.astype(jnp.bfloat16), d_inputs))
    zero_mats = jnp.zeros((D, 4 * D + 2 * FF), jnp.float32)
    zero_vecs = jnp.zeros((8 * D + FF,), jnp.float32)
    (grad_mats, grad_vecs), (outputs, input_grads) = lax.scan(one_sequence, (zero_mats, zero_vecs), (inputs_all, cotangents, segments))
    new_mats, first_mats, later_mats = adamw(mats, grad_mats, moment_mats, second_mats, rate_mats, weight_decay)
    new_vecs, first_vecs, later_vecs = adamw(vectors, grad_vecs, moment_vecs, second_vecs, rate_vecs, 0.0)
    return (outputs, input_grads, new_mats, first_mats, later_mats, new_vecs, first_vecs, later_vecs)
```

```python
import functools

import jax
import jax.numpy as jnp
from jax import lax
from jax.experimental import pallas as pl
from jax.experimental.pallas import tpu as pltpu
from jax.sharding import Mesh
from jax.sharding import PartitionSpec as P

D = 768
HEADS = 12
HEAD = D // HEADS
FF = 3072
STEP = 10
LANES = 128
PAIRS = D // LANES


norm_eps = 1e-05
first_decay = 0.9
second_decay = 0.999
adam_eps = 1e-08
rate_mats = 0.08
rate_vecs = 0.4
weight_decay = 0.01

F32 = jnp.float32
BF16 = jnp.bfloat16


def dot_nn(left, right):
    return lax.dot_general(left, right, (((1,), (0,)), ((), ())), preferred_element_type=F32)


def dot_nt(left, right):
    return lax.dot_general(left, right, (((1,), (1,)), ((), ())), preferred_element_type=F32)


def dot_tn(left, right):
    return lax.dot_general(left, right, (((0,), (0,)), ((), ())), preferred_element_type=F32)


def adamw(weight, gradient, moment, second, rate, decay):
    moment_new = first_decay * moment + (1.0 - first_decay) * gradient
    second_new = second_decay * second + (1.0 - second_decay) * gradient * gradient
    fixed_first = moment_new / (1.0 - first_decay**STEP)
    fixed_second = second_new / (1.0 - second_decay**STEP)
    weight_new = weight - rate * (
        fixed_first / (jnp.sqrt(fixed_second) + adam_eps) + decay * weight
    )
    return (weight_new, moment_new, second_new)


def attend_forward_kernel(
    q_ref, ko_ref, vo_ref, kt_ref, vt_ref, mq_ref, mo_ref, mt_ref, a_ref, e_ref, inv_ref
):
    count = q_ref.shape[0]
    own = ko_ref.shape[0]
    total = own + kt_ref.shape[0]
    q = q_ref[...]
    lane = lax.broadcasted_iota(jnp.int32, (1, LANES), 1)
    row = lax.broadcasted_iota(jnp.int32, (LANES, 1), 0)
    value_t = jnp.concatenate([vo_ref[...].T, vt_ref[...].T], axis=1)
    halves = []
    for h in range(2):
        inside = (lane < HEAD) if h == 0 else (lane >= HEAD)
        inside_row = (row < HEAD) if h == 0 else (row >= HEAD)
        q_h = jnp.where(inside, q, mq_ref[...])
        k_o = jnp.where(inside, ko_ref[...], mo_ref[...])
        k_t = jnp.where(inside, kt_ref[...], mt_ref[...])
        s_o = dot_nt(k_o, q_h)
        s_t = dot_nt(k_t, q_h)
        top = jnp.maximum(
            jnp.max(s_o, axis=0, keepdims=True), jnp.max(s_t, axis=0, keepdims=True)
        )
        e_ref[h, 0:own, :] = jnp.exp(s_o - top).astype(BF16)
        e_ref[h, own:total, :] = jnp.exp(s_t - top).astype(BF16)
        v_h = jnp.where(inside_row, value_t, jnp.ones_like(value_t))
        mixed = dot_nn(v_h, e_ref[h])
        one = HEAD if h == 0 else 0
        inverse = 1.0 / mixed[one : one + 1, :]
        inv_ref[0, h : h + 1, :] = inverse
        halves.append(mixed * inverse)
    both = jnp.where(row < HEAD, halves[0], halves[1])
    a_ref[...] = both.T.astype(BF16)


def attend_forward(q, own, other, mask_q, mask_own, mask_other):
    count = q.shape[0]
    here, there = own.shape[0], other.shape[0]
    column = lambda j: (0, j)
    shifted = lambda j: (0, j + PAIRS)
    whole = lambda j: (0, 0)
    return pl.pallas_call(
        attend_forward_kernel,
        grid=(PAIRS,),
        in_specs=[
            pl.BlockSpec((count, LANES), column),
            pl.BlockSpec((here, LANES), column),
            pl.BlockSpec((here, LANES), shifted),
            pl.BlockSpec((there, LANES), column),
            pl.BlockSpec((there, LANES), shifted),
            pl.BlockSpec((count, LANES), whole),
            pl.BlockSpec((here, LANES), whole),
            pl.BlockSpec((there, LANES), whole),
        ],
        out_specs=[
            pl.BlockSpec((count, LANES), column),
            pl.BlockSpec((2, here + there, count), lambda j: (j, 0, 0)),
            pl.BlockSpec((1, 2, count), lambda j: (j, 0, 0)),
        ],
        out_shape=[
            jax.ShapeDtypeStruct((count, D), BF16),
            jax.ShapeDtypeStruct((HEADS, here + there, count), BF16),
            jax.ShapeDtypeStruct((PAIRS, 2, count), F32),
        ],
        compiler_params=pltpu.CompilerParams(vmem_limit_bytes=40 * 2**20),
        cost_estimate=pl.CostEstimate(
            flops=16 * HEADS * HEAD * count * (here + there),
            bytes_accessed=2 * HEADS * count * (here + there),
            transcendentals=HEADS * count * (here + there),
        ),
        name="attend_forward",
    )(q, own, own, other, other, mask_q, mask_own, mask_other)


def attend_backward_kernel(
    e_ref,
    inv_ref,
    q_ref,
    ko_ref,
    vo_ref,
    kt_ref,
    vt_ref,
    a_ref,
    da_ref,
    dq_ref,
    dko_ref,
    dvo_ref,
    dkt_ref,
    dvt_ref,
    ds_ref,
):
    own = ko_ref.shape[0]
    total = own + kt_ref.shape[0]
    lane = lax.broadcasted_iota(jnp.int32, (1, LANES), 1)
    row = lax.broadcasted_iota(jnp.int32, (LANES, 1), 0)
    da = da_ref[...]
    zero = jnp.zeros_like(da)
    product = (da.astype(F32) * a_ref[...].astype(F32)).T
    inv_t = jnp.where(row < HEAD, inv_ref[0, 0:1, :], inv_ref[0, 1:2, :])
    inverse = inv_t.T
    da_scaled = (da.astype(F32) * inverse).astype(BF16)
    q_scaled = (q_ref[...].astype(F32) * inverse).astype(BF16)
    keys_t = jnp.concatenate([ko_ref[...].T, kt_ref[...].T], axis=1)
    d_value = None
    d_key = None
    halves = []
    for h in range(2):
        inside = (lane < HEAD) if h == 0 else (lane >= HEAD)
        da_h = jnp.where(inside, da, zero)
        delta = jnp.sum(product[h * HEAD : (h + 1) * HEAD, :], axis=0, keepdims=True)
        dp_o = dot_nt(vo_ref[...], da_h)
        ds_ref[h, 0:own, :] = (e_ref[h, 0:own, :].astype(F32) * (dp_o - delta)).astype(BF16)
        dp_t = dot_nt(vt_ref[...], da_h)
        ds_ref[h, own:total, :] = (
            e_ref[h, own:total, :].astype(F32) * (dp_t - delta)
        ).astype(BF16)
        part_v = dot_nn(e_ref[h], jnp.where(inside, da_scaled, zero))
        part_k = dot_nn(ds_ref[h], jnp.where(inside, q_scaled, zero))
        d_value = part_v if d_value is None else d_value + part_v
        d_key = part_k if d_key is None else d_key + part_k
        halves.append(dot_nn(keys_t, ds_ref[h]))
    both = jnp.where(row < HEAD, halves[0], halves[1]) * inv_t
    dq_ref[...] = (both.T * (HEAD**-0.5)).astype(BF16)
    dko_ref[...] = d_key[0:own].astype(BF16)
    dvo_ref[...] = d_value[0:own].astype(BF16)
    dkt_ref[...] = d_key[own:total].astype(BF16)
    dvt_ref[...] = d_value[own:total].astype(BF16)


def attend_backward(e, inverse, q, own, other, a, da):
    count = q.shape[0]
    here, there = own.shape[0], other.shape[0]
    column = lambda j: (0, j)
    shifted = lambda j: (0, j + PAIRS)
    mine = pl.BlockSpec((count, LANES), column)
    return pl.pallas_call(
        attend_backward_kernel,
        grid=(PAIRS,),
        in_specs=[
            pl.BlockSpec((2, here + there, count), lambda j: (j, 0, 0)),
            pl.BlockSpec((1, 2, count), lambda j: (j, 0, 0)),
            mine,
            pl.BlockSpec((here, LANES), column),
            pl.BlockSpec((here, LANES), shifted),
            pl.BlockSpec((there, LANES), column),
            pl.BlockSpec((there, LANES), shifted),
            mine,
            mine,
        ],
        out_specs=[
            mine,
            pl.BlockSpec((here, LANES), column),
            pl.BlockSpec((here, LANES), column),
            pl.BlockSpec((there, LANES), column),
            pl.BlockSpec((there, LANES), column),
        ],
        out_shape=[
            jax.ShapeDtypeStruct((count, D), BF16),
            jax.ShapeDtypeStruct((here, D), BF16),
            jax.ShapeDtypeStruct((here, D), BF16),
            jax.ShapeDtypeStruct((there, D), BF16),
            jax.ShapeDtypeStruct((there, D), BF16),
        ],
        scratch_shapes=[pltpu.VMEM((2, here + there, count), BF16)],
        compiler_params=pltpu.CompilerParams(vmem_limit_bytes=40 * 2**20),
        cost_estimate=pl.CostEstimate(
            flops=32 * HEADS * HEAD * count * (here + there),
            bytes_accessed=2 * HEADS * count * (here + there),
            transcendentals=0,
        ),
        name="attend_backward",
    )(e, inverse, q, own, own, other, other, a, da)


def gelu_kernel(y_ref, w_ref, b_ref, u_ref, slope_ref):
    z = dot_nt(y_ref[...], w_ref[...]) + b_ref[...]
    cdf = 0.5 + 0.5 * lax.erf(z * (0.5**0.5))
    density = jnp.exp(-0.5 * z * z) * 0.3989422804014327
    u_ref[...] = (z * cdf).astype(BF16)
    slope_ref[...] = (cdf + z * density).astype(BF16)


def gelu_layer(y, w, b, block=512):
    count = y.shape[0]
    out = pl.BlockSpec((count, block), lambda j: (0, j))
    return pl.pallas_call(
        gelu_kernel,
        grid=(FF // block,),
        in_specs=[
            pl.BlockSpec((count, D), lambda j: (0, 0)),
            pl.BlockSpec((block, D), lambda j: (j, 0)),
            pl.BlockSpec((1, block), lambda j: (0, j)),
        ],
        out_specs=[out, out],
        out_shape=[jax.ShapeDtypeStruct((count, FF), BF16)] * 2,
        compiler_params=pltpu.CompilerParams(vmem_limit_bytes=32 * 2**20),
        cost_estimate=pl.CostEstimate(
            flops=2 * count * D * FF * 2, bytes_accessed=count * FF * 4, transcendentals=count * FF
        ),
        name="gelu_layer",
    )(y, w, b)


def partners(size, offset):
    return [(i, i ^ offset) for i in range(size)]


def swap(value, axis, size, offset):
    return lax.ppermute(value, axis, partners(size, offset))


def add_low(left, right):
    return (left.astype(F32) + right.astype(F32)).astype(BF16)


def spread(value, axis, size):
    place = lax.axis_index(axis)
    offset = 1
    while offset < size:
        got = swap(value, axis, size, offset)
        low = (place // offset) % 2 == 0
        value = jnp.where(
            low, jnp.concatenate([value, got]), jnp.concatenate([got, value])
        )
        offset *= 2
    return value


def fold(value, dim, axis, size, add):
    place = lax.axis_index(axis)
    offset = size // 2
    while offset >= 1:
        half = value.shape[dim] // 2
        bit = (place // offset) % 2
        away = lax.dynamic_slice_in_dim(value, (1 - bit) * half, half, dim)
        keep = lax.dynamic_slice_in_dim(value, bit * half, half, dim)
        value = add(keep, swap(away, axis, size, offset))
        offset //= 2
    return value


def broadcast_plane(own, plane, size):
    place = lax.axis_index("z")
    value = own
    holders = [plane]
    offset = size // 2
    while offset >= 1:
        got = lax.ppermute(value, "z", [(h, h ^ offset) for h in holders])
        fresh = (place ^ plane) & offset != 0
        settled = (place ^ plane) & (offset - 1) == 0
        value = jnp.where(fresh & settled, got, value)
        holders = holders + [h ^ offset for h in holders]
        offset //= 2
    return value


def reduce_plane(value, plane, size):
    senders = list(range(size))
    offset = 1
    while offset < size:
        pairs = [(h, h ^ offset) for h in senders if (h ^ plane) & offset]
        value = add_low(value, lax.ppermute(value, "z", pairs))
        senders = [h for h in senders if not (h ^ plane) & offset]
        offset *= 2
    return value


def bundle(pieces, offsets, axis, size, step):
    offset = 1
    while offset < size:
        sent = pieces[0] if len(pieces) == 1 else jnp.concatenate(pieces)
        pieces = [sent, swap(sent, axis, size, offset)]
        offsets = offsets + [
            tuple(a ^ (offset * b) for a, b in zip(old, step)) for old in offsets
        ]
        offset *= 2
    return pieces, offsets


def gather_plane(shard, sizes, cut):
    ny, nx, nc = sizes
    found = []
    for first, last, order in ((0, cut, "xy"), (cut, shard.shape[0], "yx")):
        pieces, offsets = [shard[None, first:last]], [(0, 0)]
        for axis in order:
            size, step = (nx, (0, 1)) if axis == "x" else (ny, (1, 0))
            pieces, offsets = bundle(pieces, offsets, axis, size, step)
        for side in range(nc):
            base = 0
            for piece in pieces:
                array = piece if side == 0 else swap(piece, "core", nc, side)
                for k in range(piece.shape[0]):
                    dy, dx = offsets[base + k]
                    found.append((array, k, (dy, dx, side), first, last - first))
                base += piece.shape[0]
    return found


def assemble(found, plane, total, share, sizes, before):
    ny, nx, nc = sizes
    rows_all = share * ny * nx * nc

    def target(offset):
        dy, dx, dc = offset
        y = lax.axis_index("y") ^ dy
        x = lax.axis_index("x") ^ dx
        core = lax.axis_index("core") ^ dc
        return (y * nx + x) * nc + core

    if share % 16 != 0:
        out = jnp.zeros((total, D), BF16) if before is None else before
        for array, k, offset, first, rows in found:
            start = plane(lax.axis_index("z")) * rows_all + target(offset) * share + first
            out = lax.dynamic_update_slice(out, array[k], (start, 0))
        return out

    arrays = []
    for array, *_ in found:
        if not any(array is other for other in arrays):
            arrays.append(array)
    places = [next(i for i, o in enumerate(arrays) if o is f[0]) for f in found]

    def kernel(*refs):
        sources = refs[: len(arrays)]
        out, held, sems, last = refs[-4:]
        copies = []
        for n, (_, k, offset, first, rows) in enumerate(found):
            start = pl.multiple_of(target(offset) * share + first, 16)
            copies.append(
                pltpu.make_async_copy(
                    sources[places[n]].at[k], held.at[pl.ds(start, rows), :], sems.at[n]
                )
            )
        for copy in copies:
            copy.start()
        for copy in copies:
            copy.wait()
        base = pl.multiple_of(plane(lax.axis_index("z")) * rows_all, 16)
        copy = pltpu.make_async_copy(held, out.at[pl.ds(base, rows_all), :], last)
        copy.start()
        copy.wait()

    operands = arrays if before is None else arrays + [before]
    return pl.pallas_call(
        kernel,
        in_specs=[pl.BlockSpec(memory_space=pl.ANY)] * len(operands),
        out_specs=pl.BlockSpec(memory_space=pl.ANY),
        out_shape=jax.ShapeDtypeStruct((total, D), BF16),
        scratch_shapes=[
            pltpu.VMEM((rows_all, D), BF16),
            pltpu.SemaphoreType.DMA((len(found),)),
            pltpu.SemaphoreType.DMA,
        ],
        input_output_aliases={} if before is None else {len(arrays): 0},
        compiler_params=pltpu.CompilerParams(vmem_limit_bytes=16 * 2**20),
        cost_estimate=pl.CostEstimate(
            flops=0, bytes_accessed=4 * D * rows_all, transcendentals=0
        ),
        name="assemble",
    )(*operands)


def plane_order(size, first):
    orders = []
    for z in range(size):
        order = [z] + [p for p in range(first) if p != z]
        order += [p for p in (z ^ d for d in range(size)) if p not in order]
        orders.append(order)
    stages = []
    for stage in range(size):
        picks = [order[stage] for order in orders]
        stages.append(
            lambda z, picks=picks: sum(
                jnp.where(z == i, pick, 0) for i, pick in enumerate(picks)
            )
        )
    return stages


def tie(value, *others):
    return lax.optimization_barrier((value, *others))[0]


def norm(values, gain, shift):
    center = values - jnp.mean(values, axis=-1, keepdims=True)
    spread_ = jnp.mean(center * center, axis=-1, keepdims=True)
    rate = lax.rsqrt(spread_ + norm_eps)
    unit = center * rate
    return unit * gain + shift, unit, rate


def norm_back(cotangent, unit, rate, gain):
    scaled = cotangent * gain
    mean = jnp.mean(scaled, axis=-1, keepdims=True)
    along = jnp.mean(scaled * unit, axis=-1, keepdims=True)
    grad = rate * (scaled - mean - unit * along)
    return grad, jnp.sum(cotangent * unit, axis=0), jnp.sum(cotangent, axis=0)


def local(
    sizes,
    tokens,
    lengths,
    out_grad,
    mats,
    vectors,
    moment_mats,
    second_mats,
    moment_vecs,
    second_vecs,
):
    nz, ny, nx, nc = sizes
    flat = (ny, nx, nc)
    sequences, span, _ = tokens.shape
    share = mats.shape[1]
    plane_rows = share * ny * nx * nc
    first_planes = 3 * D // plane_rows
    cut = share * 2 // 3 // 16 * 16
    x_place, core = lax.axis_index("x"), lax.axis_index("core")
    half = nx // 2
    side = x_place // half

    def regroup(value):
        mine = lax.dynamic_index_in_dim(value, side, 0, keepdims=False)
        away = lax.dynamic_index_in_dim(value, 1 - side, 0, keepdims=False)
        return mine, away

    def far(value):
        return swap(value, "x", nx, half)

    def ungroup(mine, got):
        low, high = (jnp.stack([mine, got]), jnp.stack([got, mine]))
        return jnp.where(side == 0, low, high)

    mine, away = regroup(tokens)
    inputs = jnp.concatenate([mine, far(away)])
    count = inputs.shape[0]

    shard = mats.T.astype(BF16)
    vec = jnp.pad(vectors, (0, -share % 1024)).reshape(1, -1, 128)
    vec = vec.astype(BF16)
    for axis, size in (("core", nc), ("x", nx), ("y", ny), ("z", nz)):
        vec = spread(vec, axis, size)
    biases = vec.reshape(vec.shape[0], -1)[:, :share].reshape(-1).astype(F32)
    shards = []
    for plane in range(nz):
        shards.append(broadcast_plane(shard, plane, nz))
    shards = jnp.stack(shards)
    z_place = lax.axis_index("z")
    rows = None
    w_qkv = None
    for stage, plane in enumerate(plane_order(nz, first_planes)):
        block = shard
        if stage > 0:
            block = lax.dynamic_index_in_dim(shards, plane(z_place), 0, keepdims=False)
        found = gather_plane(block, flat, cut)
        rows = assemble(found, plane, nz * plane_rows, share, flat, rows)
        if stage == first_planes:
            w_qkv, rows = lax.optimization_barrier((rows[: 3 * D], rows))
    high_rows = rows[3 * D :]
    w_out = high_rows[0:D]
    w_first = high_rows[D : D + FF]
    w_second = high_rows[D + FF :]
    b_query = biases[0:D]
    b_value = biases[D : 2 * D]
    b_out = biases[2 * D : 3 * D]
    gain_one = biases[3 * D : 4 * D]
    shift_one = biases[4 * D : 5 * D]
    gain_two = biases[5 * D : 6 * D]
    shift_two = biases[6 * D : 7 * D]
    b_second = biases[7 * D : 8 * D]
    b_first = biases[8 * D :]

    ends = jnp.cumsum(lax.dynamic_index_in_dim(lengths, side, 0, keepdims=False))

    def documents(offset_x, offset_core):
        at = lax.broadcasted_iota(jnp.int32, (2, span), 1)
        part = lax.broadcasted_iota(jnp.int32, (2, span), 0)
        x_at = x_place ^ offset_x ^ (part * half)
        at = ((x_at * nc) + (core ^ offset_core)) * span + at
        at = at.reshape(-1, 1)
        return jnp.sum((at >= ends[None, :]).astype(jnp.int32), axis=-1, keepdims=True)

    slot = lax.broadcasted_iota(jnp.int32, (1, LANES), 1) % HEAD
    group = [(dx, dc) for dx in range(half) for dc in range(nc)]
    seg = [documents(dx, dc) for dx, dc in group]
    mask_q = jnp.where(slot == seg[0], -1e30, 0.0).astype(BF16)
    mask_own = (slot != seg[0]).astype(BF16)
    mask_other = (slot != jnp.concatenate(seg[1:])).astype(BF16)

    key_value = dot_nt(inputs, w_qkv[D:])
    key_value = (key_value + jnp.concatenate([jnp.zeros_like(b_value), b_value])).astype(BF16)
    pieces = [key_value, swap(key_value, "core", nc, 1)]
    offset = 1
    while offset < half:
        sent = jnp.concatenate(pieces)
        got = swap(sent, "x", nx, offset)
        pieces = [pieces[0], jnp.concatenate([sent[count:], got])]
        offset *= 2
    own, other = pieces
    query = ((dot_nt(inputs, w_qkv[:D]) + b_query).astype(BF16).astype(F32) * HEAD**-0.5).astype(
        BF16
    )
    mixed, exponents, inverse = attend_forward(query, own, other, mask_q, mask_own, mask_other)

    inputs_wide = inputs.astype(F32)
    hidden = inputs_wide + dot_nt(mixed, w_out) + b_out
    normed, unit_one, rate_one = norm(hidden, gain_one, shift_one)
    normed_low = normed.astype(BF16)
    active, slope = gelu_layer(normed_low, w_first, b_first.reshape(1, -1))
    hidden_two = normed + dot_nn(active, w_second) + b_second
    result, unit_two, rate_two = norm(hidden_two, gain_two, shift_two)
    result = result.astype(BF16)
    block_out = ungroup(result[:span], far(result[span:]))

    mine, away = regroup(out_grad)
    cotangent = jnp.concatenate([mine, far(away)]).astype(F32)
    d_hidden_two, d_gain_two, d_shift_two = norm_back(cotangent, unit_two, rate_two, gain_two)
    d_feed = d_hidden_two.astype(BF16)
    d_b_second = jnp.sum(d_feed.astype(F32), axis=0)
    d_w_second = dot_tn(active, d_feed).astype(BF16)
    d_inner = (dot_nt(d_feed, w_second) * slope.astype(F32)).astype(BF16)
    d_b_first = jnp.sum(d_inner.astype(F32), axis=0)
    d_w_first = dot_tn(d_inner, normed_low).astype(BF16)
    d_normed = d_hidden_two + dot_nn(d_inner, w_first)
    d_hidden, d_gain_one, d_shift_one = norm_back(d_normed, unit_one, rate_one, gain_one)
    d_branch = d_hidden.astype(BF16)
    d_b_out = jnp.sum(d_branch.astype(F32), axis=0)
    d_w_out = dot_tn(d_branch, mixed).astype(BF16)
    d_mixed = dot_nn(d_branch, w_out).astype(BF16)

    d_query, d_key_own, d_value_own, d_key_other, d_value_other = attend_backward(
        exponents, inverse, query, own, other, mixed, d_mixed
    )
    d_own = jnp.concatenate([d_key_own, d_value_own], axis=1)
    d_other = jnp.concatenate([d_key_other, d_value_other], axis=1)
    offset = half // 2
    while offset >= 1:
        rows = offset * nc * count
        got = swap(d_other[rows - count :], "x", nx, offset)
        d_own = add_low(d_own, got[:count])
        d_other = add_low(d_other[: rows - count], got[count:])
        offset //= 2
    d_key_value = add_low(d_own, swap(d_other, "core", nc, 1))
    d_projected = jnp.concatenate([d_query, d_key_value], axis=1)
    d_w_qkv = dot_tn(d_projected, inputs).astype(BF16)
    d_b_query = jnp.sum(d_query.astype(F32), axis=0)
    d_b_value = jnp.sum(d_key_value[:, D:].astype(F32), axis=0)
    d_inputs = d_hidden + dot_nn(d_projected, w_qkv)
    d_away = far(d_inputs[span:].astype(BF16)).astype(F32)
    input_grad = ungroup(d_inputs[:span], d_away)

    grad_high = jnp.concatenate([d_w_out, d_w_first, d_w_second])
    own_mats = jnp.zeros((share, D), F32)
    for plane in reversed(range(nz)):
        if plane < first_planes:
            block = d_w_qkv[plane * plane_rows : (plane + 1) * plane_rows]
        else:
            start = (plane - first_planes) * plane_rows
            block = grad_high[start : start + plane_rows]
        block = block.reshape(ny * nx, nc, share, D)
        block = fold(block, 1, "core", nc, add_low).reshape(ny, nx, share, D)
        upper = fold(block[:, :, :cut], 0, "y", ny, add_low)
        upper = fold(upper, 1, "x", nx, add_low)
        lower = fold(block[:, :, cut:], 1, "x", nx, add_low)
        lower = fold(lower, 0, "y", ny, add_low)
        block = jnp.concatenate([upper.reshape(-1, D), lower.reshape(-1, D)])
        block = reduce_plane(block, plane, nz)
        own_mats = jnp.where(z_place == plane, block.astype(F32), own_mats)

    grad_vecs = jnp.concatenate(
        [
            d_b_query,
            d_b_value,
            d_b_out,
            d_gain_one,
            d_shift_one,
            d_gain_two,
            d_shift_two,
            d_b_second,
            d_b_first,
        ]
    ).reshape(-1, share)
    grad_vecs = jnp.pad(grad_vecs, ((0, 0), (0, -share % 1024))).reshape(
        grad_vecs.shape[0], -1, 128
    )
    for axis, size in (("z", nz), ("y", ny), ("x", nx), ("core", nc)):
        grad_vecs = fold(grad_vecs, 0, axis, size, jnp.add)
    own_vecs = grad_vecs.reshape(-1)[:share]

    new_mats, first_mats, later_mats = adamw(
        mats, own_mats.T, moment_mats, second_mats, rate_mats, weight_decay
    )
    new_vecs, first_vecs, later_vecs = adamw(
        vectors, own_vecs, moment_vecs, second_vecs, rate_vecs, 0.0
    )
    return (
        block_out,
        input_grad,
        new_mats,
        first_mats,
        later_mats,
        new_vecs,
        first_vecs,
        later_vecs,
    )


def solution(mesh):
    dp, seq = mesh.shape["dp"], mesh.shape["seq"]
    ny = 2 ** ((dp.bit_length() - 1) // 2)
    sizes = (dp // ny, ny, seq // 2, 2)
    fine = Mesh(mesh.devices.reshape(sizes), ("z", "y", "x", "core"))
    rows, every = ("z", "y"), ("z", "y", "x", "core")
    tokens = P(rows, ("x", "core"), None)
    return jax.shard_map(
        functools.partial(local, sizes),
        mesh=fine,
        in_specs=(
            tokens,
            P(rows, None),
            tokens,
            P(None, every),
            P(every),
            P(None, every),
            P(None, every),
            P(every),
            P(every),
        ),
        out_specs=(
            tokens,
            tokens,
            P(None, every),
            P(None, every),
            P(None, every),
            P(every),
            P(every),
            P(every),
        ),
        check_vma=False,
    )
```

```python
import functools

import jax
import jax.numpy as jnp
from jax import lax
from jax.experimental import pallas as pl
from jax.experimental.pallas import tpu as pltpu
from jax.sharding import Mesh
from jax.sharding import PartitionSpec as P

D = 768
HEADS = 12
HEAD = D // HEADS
FF = 3072
STEP = 10
LANES = 128
PAIRS = D // LANES


norm_eps = 1e-05
first_decay = 0.9
second_decay = 0.999
adam_eps = 1e-08
rate_mats = 0.08
rate_vecs = 0.4
weight_decay = 0.01

F32 = jnp.float32
BF16 = jnp.bfloat16


def dot_nn(left, right):
    return lax.dot_general(left, right, (((1,), (0,)), ((), ())), preferred_element_type=F32)


def dot_nt(left, right):
    return lax.dot_general(left, right, (((1,), (1,)), ((), ())), preferred_element_type=F32)


def dot_tn(left, right):
    return lax.dot_general(left, right, (((0,), (0,)), ((), ())), preferred_element_type=F32)


def adamw(weight, gradient, moment, second, rate, decay):
    moment_new = first_decay * moment + (1.0 - first_decay) * gradient
    second_new = second_decay * second + (1.0 - second_decay) * gradient * gradient
    fixed_first = moment_new / (1.0 - first_decay**STEP)
    fixed_second = second_new / (1.0 - second_decay**STEP)
    weight_new = weight - rate * (
        fixed_first / (jnp.sqrt(fixed_second) + adam_eps) + decay * weight
    )
    return (weight_new, moment_new, second_new)


def attend_forward_kernel(
    q_ref, ko_ref, vo_ref, kt_ref, vt_ref, mq_ref, mo_ref, mt_ref, a_ref, e_ref, inv_ref
):
    count = q_ref.shape[0]
    own = ko_ref.shape[0]
    total = own + kt_ref.shape[0]
    q = q_ref[...]
    lane = lax.broadcasted_iota(jnp.int32, (1, LANES), 1)
    row = lax.broadcasted_iota(jnp.int32, (LANES, 1), 0)
    value_t = jnp.concatenate([vo_ref[...].T, vt_ref[...].T], axis=1)
    halves = []
    for h in range(2):
        inside = (lane < HEAD) if h == 0 else (lane >= HEAD)
        inside_row = (row < HEAD) if h == 0 else (row >= HEAD)
        q_h = jnp.where(inside, q, mq_ref[...])
        k_o = jnp.where(inside, ko_ref[...], mo_ref[...])
        k_t = jnp.where(inside, kt_ref[...], mt_ref[...])
        s_o = dot_nt(k_o, q_h)
        s_t = dot_nt(k_t, q_h)
        top = jnp.maximum(
            jnp.max(s_o, axis=0, keepdims=True), jnp.max(s_t, axis=0, keepdims=True)
        )
        e_ref[h, 0:own, :] = jnp.exp(s_o - top).astype(BF16)
        e_ref[h, own:total, :] = jnp.exp(s_t - top).astype(BF16)
        v_h = jnp.where(inside_row, value_t, jnp.ones_like(value_t))
        mixed = dot_nn(v_h, e_ref[h])
        one = HEAD if h == 0 else 0
        inverse = 1.0 / mixed[one : one + 1, :]
        inv_ref[0, h : h + 1, :] = inverse
        halves.append(mixed * inverse)
    both = jnp.where(row < HEAD, halves[0], halves[1])
    a_ref[...] = both.T.astype(BF16)


def attend_forward(q, own, other, mask_q, mask_own, mask_other, first, pairs):
    count = q.shape[0]
    here, there = own.shape[0], other.shape[0]
    place = lambda j: (0, j)
    column = lambda j: (0, j + first)
    shifted = lambda j: (0, j + first + PAIRS)
    whole = lambda j: (0, 0)
    return pl.pallas_call(
        attend_forward_kernel,
        grid=(pairs,),
        in_specs=[
            pl.BlockSpec((count, LANES), column),
            pl.BlockSpec((here, LANES), column),
            pl.BlockSpec((here, LANES), shifted),
            pl.BlockSpec((there, LANES), column),
            pl.BlockSpec((there, LANES), shifted),
            pl.BlockSpec((count, LANES), whole),
            pl.BlockSpec((here, LANES), whole),
            pl.BlockSpec((there, LANES), whole),
        ],
        out_specs=[
            pl.BlockSpec((count, LANES), place),
            pl.BlockSpec((2, here + there, count), lambda j: (j, 0, 0)),
            pl.BlockSpec((1, 2, count), lambda j: (j, 0, 0)),
        ],
        out_shape=[
            jax.ShapeDtypeStruct((count, pairs * LANES), BF16),
            jax.ShapeDtypeStruct((2 * pairs, here + there, count), BF16),
            jax.ShapeDtypeStruct((pairs, 2, count), F32),
        ],
        compiler_params=pltpu.CompilerParams(vmem_limit_bytes=40 * 2**20),
        cost_estimate=pl.CostEstimate(
            flops=32 * pairs * HEAD * count * (here + there),
            bytes_accessed=4 * pairs * count * (here + there),
            transcendentals=2 * pairs * count * (here + there),
        ),
        name="attend_forward",
    )(q, own, own, other, other, mask_q, mask_own, mask_other)


def attend_backward_kernel(
    e_ref,
    inv_ref,
    q_ref,
    ko_ref,
    vo_ref,
    kt_ref,
    vt_ref,
    a_ref,
    da_ref,
    dq_ref,
    dko_ref,
    dvo_ref,
    dkt_ref,
    dvt_ref,
    ds_ref,
):
    own = ko_ref.shape[0]
    total = own + kt_ref.shape[0]
    lane = lax.broadcasted_iota(jnp.int32, (1, LANES), 1)
    row = lax.broadcasted_iota(jnp.int32, (LANES, 1), 0)
    da = da_ref[...]
    zero = jnp.zeros_like(da)
    product = (da.astype(F32) * a_ref[...].astype(F32)).T
    inv_t = jnp.where(row < HEAD, inv_ref[0, 0:1, :], inv_ref[0, 1:2, :])
    inverse = inv_t.T
    da_scaled = (da.astype(F32) * inverse).astype(BF16)
    q_scaled = (q_ref[...].astype(F32) * inverse).astype(BF16)
    keys_t = jnp.concatenate([ko_ref[...].T, kt_ref[...].T], axis=1)
    d_value = None
    d_key = None
    halves = []
    for h in range(2):
        inside = (lane < HEAD) if h == 0 else (lane >= HEAD)
        da_h = jnp.where(inside, da, zero)
        delta = jnp.sum(product[h * HEAD : (h + 1) * HEAD, :], axis=0, keepdims=True)
        dp_o = dot_nt(vo_ref[...], da_h)
        ds_ref[h, 0:own, :] = (e_ref[h, 0:own, :].astype(F32) * (dp_o - delta)).astype(BF16)
        dp_t = dot_nt(vt_ref[...], da_h)
        ds_ref[h, own:total, :] = (
            e_ref[h, own:total, :].astype(F32) * (dp_t - delta)
        ).astype(BF16)
        part_v = dot_nn(e_ref[h], jnp.where(inside, da_scaled, zero))
        part_k = dot_nn(ds_ref[h], jnp.where(inside, q_scaled, zero))
        d_value = part_v if d_value is None else d_value + part_v
        d_key = part_k if d_key is None else d_key + part_k
        halves.append(dot_nn(keys_t, ds_ref[h]))
    both = jnp.where(row < HEAD, halves[0], halves[1]) * inv_t
    dq_ref[...] = (both.T * (HEAD**-0.5)).astype(BF16)
    dko_ref[...] = d_key[0:own].astype(BF16)
    dvo_ref[...] = d_value[0:own].astype(BF16)
    dkt_ref[...] = d_key[own:total].astype(BF16)
    dvt_ref[...] = d_value[own:total].astype(BF16)


def attend_backward(e, inverse, q, own, other, a, da, first, pairs):
    count = q.shape[0]
    here, there = own.shape[0], other.shape[0]
    place = lambda j: (0, j)
    column = lambda j: (0, j + first)
    shifted = lambda j: (0, j + first + PAIRS)
    mine = pl.BlockSpec((count, LANES), column)
    width = pairs * LANES
    return pl.pallas_call(
        attend_backward_kernel,
        grid=(pairs,),
        in_specs=[
            pl.BlockSpec((2, here + there, count), lambda j: (j, 0, 0)),
            pl.BlockSpec((1, 2, count), lambda j: (j, 0, 0)),
            mine,
            pl.BlockSpec((here, LANES), column),
            pl.BlockSpec((here, LANES), shifted),
            pl.BlockSpec((there, LANES), column),
            pl.BlockSpec((there, LANES), shifted),
            pl.BlockSpec((count, LANES), place),
            mine,
        ],
        out_specs=[
            pl.BlockSpec((count, LANES), place),
            pl.BlockSpec((here, LANES), place),
            pl.BlockSpec((here, LANES), place),
            pl.BlockSpec((there, LANES), place),
            pl.BlockSpec((there, LANES), place),
        ],
        out_shape=[
            jax.ShapeDtypeStruct((count, width), BF16),
            jax.ShapeDtypeStruct((here, width), BF16),
            jax.ShapeDtypeStruct((here, width), BF16),
            jax.ShapeDtypeStruct((there, width), BF16),
            jax.ShapeDtypeStruct((there, width), BF16),
        ],
        scratch_shapes=[pltpu.VMEM((2, here + there, count), BF16)],
        compiler_params=pltpu.CompilerParams(vmem_limit_bytes=40 * 2**20),
        cost_estimate=pl.CostEstimate(
            flops=64 * pairs * HEAD * count * (here + there),
            bytes_accessed=4 * pairs * count * (here + there),
            transcendentals=0,
        ),
        name="attend_backward",
    )(e, inverse, q, own, own, other, other, a, da)


def gelu_kernel(y_ref, w_ref, b_ref, u_ref, slope_ref):
    z = dot_nt(y_ref[...], w_ref[...]) + b_ref[...]
    cdf = 0.5 + 0.5 * lax.erf(z * (0.5**0.5))
    density = jnp.exp(-0.5 * z * z) * 0.3989422804014327
    u_ref[...] = (z * cdf).astype(BF16)
    slope_ref[...] = (cdf + z * density).astype(BF16)


def gelu_layer(y, rows, b, first):
    count, block = y.shape[0], D
    out = pl.BlockSpec((count, block), lambda j: (0, j))
    return pl.pallas_call(
        gelu_kernel,
        grid=(FF // block,),
        in_specs=[
            pl.BlockSpec((count, D), lambda j: (0, 0)),
            pl.BlockSpec((block, D), lambda j: (j + first // block, 0)),
            pl.BlockSpec((1, block), lambda j: (0, j)),
        ],
        out_specs=[out, out],
        out_shape=[jax.ShapeDtypeStruct((count, FF), BF16)] * 2,
        compiler_params=pltpu.CompilerParams(vmem_limit_bytes=32 * 2**20),
        cost_estimate=pl.CostEstimate(
            flops=2 * count * D * FF * 2, bytes_accessed=count * FF * 4, transcendentals=count * FF
        ),
        name="gelu_layer",
    )(y, rows, b)


def partners(size, offset):
    return [(i, i ^ offset) for i in range(size)]


def swap(value, axis, size, offset):
    return lax.ppermute(value, axis, partners(size, offset))


def add_low(left, right):
    return (left.astype(F32) + right.astype(F32)).astype(BF16)


def tie(value, *others):
    return lax.optimization_barrier((value, *others))[0]


def fold(value, dim, axis, size, add):
    place = lax.axis_index(axis)
    offset = size // 2
    while offset >= 1:
        half = value.shape[dim] // 2
        bit = (place // offset) % 2
        away = lax.dynamic_slice_in_dim(value, (1 - bit) * half, half, dim)
        keep = lax.dynamic_slice_in_dim(value, bit * half, half, dim)
        value = add(keep, swap(away, axis, size, offset))
        offset //= 2
    return value


def broadcast_planes(own, size):
    place = lax.axis_index("z")
    values = [own] * size
    offset = size // 2
    order = [0, size // 2] + [p for p in range(1, size) if p != size // 2]
    step = size
    while offset >= 1:
        lead = None
        for plane in order:
            value = values[plane]
            if plane != 0 and (plane != size // 2 or step < size):
                value = tie(value, lead)
            holders = [h for h in range(size) if (h ^ plane) & (2 * offset - 1) == 0]
            got = lax.ppermute(value, "z", [(h, h ^ offset) for h in holders])
            fresh = (place ^ plane) & (2 * offset - 1) == offset
            values[plane] = jnp.where(fresh, got, value)
            if plane == 0:
                lead = values[0]
        step = offset
        offset //= 2
    return values


def reduce_plane(value, plane, size):
    senders = list(range(size))
    offset = 1
    while offset < size:
        pairs = [(h, h ^ offset) for h in senders if (h ^ plane) & offset]
        value = add_low(value, lax.ppermute(value, "z", pairs))
        senders = [h for h in senders if not (h ^ plane) & offset]
        offset *= 2
    return value


def bundle(pieces, offsets, axis, size, step):
    offset = 1
    while offset < size:
        sent = pieces[0] if len(pieces) == 1 else jnp.concatenate(pieces)
        pieces = [sent, swap(sent, axis, size, offset)]
        offsets = offsets + [
            tuple(a ^ (offset * b) for a, b in zip(old, step)) for old in offsets
        ]
        offset *= 2
    return pieces, offsets


def gather_plane(shard, sizes, cut):
    ny, nx, nc = sizes
    found, early, late = [], [], []
    for first, last, order in ((0, cut, "xy"), (cut, shard.shape[0], "yx")):
        pieces, offsets = [shard[None, first:last]], [(0, 0)]
        for axis in order:
            size, step = (nx, (0, 1)) if axis == "x" else (ny, (1, 0))
            pieces, offsets = bundle(pieces, offsets, axis, size, step)
            (early if axis == order[0] else late).append(pieces[-1])
        for side in range(nc):
            base = 0
            for piece in pieces:
                array = piece if side == 0 else swap(piece, "core", nc, side)
                for k in range(piece.shape[0]):
                    dy, dx = offsets[base + k]
                    found.append((array, k, (dy, dx, side), first))
                base += piece.shape[0]
    return found, early, late


def assemble(found, plane, counts, share, sizes, before):
    ny, nx, nc = sizes
    owners = ny * nx * nc
    rows_all = share * owners
    planes, first_planes = counts
    shapes = [
        (first_planes * rows_all, D),
        ((planes - first_planes) * rows_all, D),
        (planes * owners * 16, D),
    ]

    def target(offset):
        dy, dx, dc = offset
        y = lax.axis_index("y") ^ dy
        x = lax.axis_index("x") ^ dx
        core = lax.axis_index("core") ^ dc
        return (y * nx + x) * nc + core

    if share % 16 != 0:
        low, high, vecs = before or [jnp.zeros(shape, BF16) for shape in shapes]
        rows = jnp.concatenate([low, high])
        base = plane(lax.axis_index("z"))
        for array, k, offset, first in found:
            count = min(array.shape[1], share - first)
            start = base * rows_all + target(offset) * share + first
            rows = lax.dynamic_update_slice(rows, array[k, :count], (start, 0))
            if count < array.shape[1]:
                start = (base * owners + target(offset)) * 16
                vecs = lax.dynamic_update_slice(vecs, array[k, count:], (start, 0))
        return [rows[: first_planes * rows_all], rows[first_planes * rows_all :], vecs]

    arrays = []
    for array, *_ in found:
        if not any(array is other for other in arrays):
            arrays.append(array)
    places = [next(i for i, o in enumerate(arrays) if o is f[0]) for f in found]
    before = before or []
    outs = shapes if len(before) != 2 else shapes[1:]

    def kernel(*refs):
        sources = refs[: len(arrays)]
        results = refs[len(arrays) + len(before) :][: len(outs)]
        held, held_vec, sems, sems_vec, last = refs[-5:]
        copies, copies_vec = [], []
        for n, (array, k, offset, first) in enumerate(found):
            count = min(array.shape[1], share - first)
            source = sources[places[n]]
            start = pl.multiple_of(target(offset) * share + first, 16)
            copies.append(
                pltpu.make_async_copy(
                    source.at[k, pl.ds(0, count), :],
                    held.at[pl.ds(start, count), :],
                    sems.at[n],
                )
            )
            if count < array.shape[1]:
                start = pl.multiple_of(target(offset) * 16, 16)
                copies_vec.append(
                    pltpu.make_async_copy(
                        source.at[k, pl.ds(count, 16), :],
                        held_vec.at[pl.ds(start, 16), :],
                        sems_vec.at[n],
                    )
                )
        for copy in copies + copies_vec:
            copy.start()
        z = plane(lax.axis_index("z"))
        is_first = z < first_planes

        def write(out, index):
            writes = []
            for n, (array, _, offset, first) in enumerate(found):
                count = min(array.shape[1], share - first)
                start = target(offset) * share + first
                base = pl.multiple_of(index * rows_all + start, 16)
                start = pl.multiple_of(start, 16)
                copies[n].wait()
                writes.append(
                    pltpu.make_async_copy(
                        held.at[pl.ds(start, count), :],
                        out.at[pl.ds(base, count), :],
                        last.at[n],
                    )
                )
                writes[-1].start()
            for copy in copies_vec:
                copy.wait()
            base = pl.multiple_of(z * owners * 16, 16)
            writes.append(
                pltpu.make_async_copy(
                    held_vec,
                    results[-1].at[pl.ds(base, owners * 16), :],
                    last.at[len(found)],
                )
            )
            writes[-1].start()
            for copy in writes:
                copy.wait()

        if len(outs) == 3:

            @pl.when(is_first)
            def _():
                write(results[0], jnp.minimum(z, first_planes - 1))

            @pl.when(jnp.logical_not(is_first))
            def _():
                write(results[1], jnp.maximum(z - first_planes, 0))

        else:
            write(results[0], z - first_planes)

    operands = arrays + list(before)
    anywhere = pl.BlockSpec(memory_space=pl.ANY)
    return pl.pallas_call(
        kernel,
        in_specs=[anywhere] * len(operands),
        out_specs=[anywhere] * len(outs),
        out_shape=[jax.ShapeDtypeStruct(shape, BF16) for shape in outs],
        scratch_shapes=[
            pltpu.VMEM((rows_all, D), BF16),
            pltpu.VMEM((owners * 16, D), BF16),
            pltpu.SemaphoreType.DMA((len(found),)),
            pltpu.SemaphoreType.DMA((len(found),)),
            pltpu.SemaphoreType.DMA((len(found) + 1,)),
        ],
        input_output_aliases={len(arrays) + i: i for i in range(len(before))},
        compiler_params=pltpu.CompilerParams(vmem_limit_bytes=52 * 2**20),
        cost_estimate=pl.CostEstimate(
            flops=0, bytes_accessed=4 * D * rows_all, transcendentals=0
        ),
        name="assemble",
    )(*operands)


def plane_start(block, cut):
    return {"parts": [block[None, :cut], block[None, cut:]]}


def plane_first(plane):
    upper, lower = plane["parts"]
    plane["got"] = [swap(upper, "x", 2, 1), swap(lower, "y", 2, 1)]


def plane_second(plane):
    pairs = [jnp.concatenate(both) for both in zip(plane.pop("parts"), plane.pop("got"))]
    plane["own"] = pairs + [swap(pairs[0], "y", 2, 1), swap(pairs[1], "x", 2, 1)]


def plane_cores(plane):
    plane["other"] = [swap(array, "core", 2, 1) for array in plane["own"]]


def plane_found(plane, cut):
    places = [((0, 0), (0, 1)), ((0, 0), (1, 0)), ((1, 0), (1, 1)), ((0, 1), (1, 1))]
    found = []
    for core, arrays in enumerate((plane["own"], plane["other"])):
        for n, (array, offsets) in enumerate(zip(arrays, places)):
            for k, offset in enumerate(offsets):
                found.append((array, k, (*offset, core), 0 if n % 2 == 0 else cut))
    return found


def fence(live):
    return lax.optimization_barrier(live)


def take(value, index, dim):
    return lax.dynamic_index_in_dim(value, index, dim, keepdims=False)


def half_send(value, dim, axis, whole=None):
    place = lax.axis_index(axis)
    away = take(value, 1 - place, dim)
    if whole is None:
        return {"all": value, "got": swap(away, axis, 2, 1)}
    rows = jnp.concatenate([away.reshape(-1, D), whole])
    got = swap(rows, axis, 2, 1)
    return {"all": value, "got": got[:-16].reshape(away.shape), "whole": got[-16:]}


def half_add(sent, dim, axis):
    return add_low(take(sent["all"], lax.axis_index(axis), dim), sent["got"])


def plane_order(size, first):
    orders = []
    for z in range(size):
        order = [z] + [p for p in range(first) if p != z]
        shifts = sorted(range(size), key=lambda d: -(d & -d))
        order += [p for p in (z ^ d for d in shifts) if p not in order]
        orders.append(order)
    return [[order[stage] for order in orders] for stage in range(size)]


def pick(picks):
    return lambda z: sum(jnp.where(z == i, p, 0) for i, p in enumerate(picks))


def norm(values, gain, shift):
    center = values - jnp.mean(values, axis=-1, keepdims=True)
    spread_ = jnp.mean(center * center, axis=-1, keepdims=True)
    rate = lax.rsqrt(spread_ + norm_eps)
    unit = center * rate
    return unit * gain + shift, unit, rate


def norm_back(cotangent, unit, rate, gain):
    scaled = cotangent * gain
    mean = jnp.mean(scaled, axis=-1, keepdims=True)
    along = jnp.mean(scaled * unit, axis=-1, keepdims=True)
    grad = rate * (scaled - mean - unit * along)
    return grad, jnp.sum(cotangent * unit, axis=0), jnp.sum(cotangent, axis=0)


def local(
    sizes,
    tokens,
    lengths,
    out_grad,
    mats,
    vectors,
    moment_mats,
    second_mats,
    moment_vecs,
    second_vecs,
):
    nz, ny, nx, nc = sizes
    flat = (ny, nx, nc)
    sequences, span, _ = tokens.shape
    share = mats.shape[1]
    plane_rows = share * ny * nx * nc
    first_planes = 3 * D // plane_rows
    cut = share // 2 // 16 * 16
    x_place, core = lax.axis_index("x"), lax.axis_index("core")
    half = nx // 2
    side = x_place // half

    def regroup(value):
        mine = lax.dynamic_index_in_dim(value, side, 0, keepdims=False)
        away = lax.dynamic_index_in_dim(value, 1 - side, 0, keepdims=False)
        return mine, away

    def far(value):
        return swap(value, "x", nx, half)

    def ungroup(mine, got):
        low, high = (jnp.stack([mine, got]), jnp.stack([got, mine]))
        return jnp.where(side == 0, low, high)

    count = sequences * span

    vec = jnp.pad(vectors.reshape(1, share), ((0, 15), (0, D - share)))
    shard = jnp.concatenate([mats.T.astype(BF16), vec.astype(BF16)])
    z_place = lax.axis_index("z")
    counts = (nz, first_planes)

    def vectors_of(store):
        low = store[-1].reshape(-1, 16, D)[:, 0, :share]
        return low.reshape(-1).astype(F32)

    token_mine, token_away = regroup(tokens)
    grad_mine, grad_away = regroup(out_grad)

    def project_key_value(inputs, rows, vec):
        key_value = dot_nt(inputs, rows[D : 3 * D])
        b_value = vec[D : 2 * D]
        return (key_value + jnp.concatenate([jnp.zeros_like(b_value), b_value])).astype(BF16)

    def project_query(inputs, rows, vec):
        query = (dot_nt(inputs, rows[:D]) + vec[:D]).astype(BF16)
        return (query.astype(F32) * HEAD**-0.5).astype(BF16)

    if sizes == (4, 2, 2, 2):
        odd = z_place % 2 == 1
        orders = [[0, 1, 2, 3], [2, 0, 0, 0], [1, 3, 3, 1], [3, 2, 1, 2]]

        def placed(live, n, store):
            return assemble(
                plane_found(live[f"w{n}"], cut), pick(orders[n]), counts, share, flat, store
            )

        live = {"shard": shard, "w0": plane_start(shard, cut), "grad_away": grad_away}
        live["z_one"] = lax.ppermute(shard, "z", [(0, 2), (2, 0)])
        plane_first(live["w0"])
        live["token_far"] = far(token_away)
        live = fence(live)

        live["z_two"] = swap(
            jnp.where(z_place == 2, live["z_one"], live["shard"]), "z", 4, 1
        )
        plane_second(live["w0"])
        live = fence(live)

        live["w1"] = plane_start(jnp.where(odd, live["z_two"], live["z_one"]), cut)
        live["z_three"] = lax.ppermute(live["shard"], "z", [(1, 3), (3, 1)])
        plane_first(live["w1"])
        plane_second(live["w1"])
        plane_cores(live["w0"])
        live = fence(live)

        even_part = jnp.where(z_place == 0, live.pop("z_one"), live.pop("shard"))
        live["z_four"] = swap(jnp.where(odd, live["z_three"], even_part), "z", 4, 1)
        live["w2"] = plane_start(jnp.where(odd, live.pop("z_three"), live.pop("z_two")), cut)
        plane_first(live["w2"])
        plane_second(live["w2"])
        plane_cores(live["w1"])
        live["store"] = placed(live, 0, None)
        del live["w0"]
        live["inputs"] = jnp.concatenate([token_mine, live.pop("token_far")])
        live = fence(live)

        live["w3"] = plane_start(live.pop("z_four"), cut)
        plane_first(live["w3"])
        plane_second(live["w3"])
        plane_cores(live["w2"])
        store = placed(live, 1, live.pop("store"))
        del live["w1"]
        first_vec = vectors_of(store)
        live["low_rows"], live["store"] = store[0], store[1:]
        live["key_value"] = project_key_value(live["inputs"], store[0], first_vec)
        live["query"] = project_query(live["inputs"], store[0], first_vec)
        live = fence(live)

        live["kv_got"] = swap(live["key_value"], "core", nc, 1)
        plane_cores(live["w3"])
        live["store"] = placed(live, 2, live.pop("store"))
        del live["w2"]
        live = fence(live)

        grad_far = far(live.pop("grad_away"))
        inputs, low_rows, query = live["inputs"], live["low_rows"], live["query"]
        own, other = live["key_value"], live["kv_got"]
        store = placed(live, 3, live["store"])
    else:
        token_far, grad_far = far(token_away), far(grad_away)
        shards = broadcast_planes(shard, nz)
        store, gates, waits = None, [], []
        for stage, picks in enumerate(plane_order(nz, first_planes)):
            plane = pick(picks)
            block = shards[picks[0]]
            for p in sorted(set(picks[1:])):
                block = jnp.where(plane(z_place) == p, shards[p], block)
            block = tie(block, *gates) if gates else block
            found, early, late = gather_plane(block, flat, cut)
            gates = early + waits
            waits = late
            store = assemble(found, plane, counts, share, flat, store)
            if stage == first_planes:
                first_vec = vectors_of(store)
                low_rows, store = store[0], store
        inputs = jnp.concatenate([token_mine, token_far])
        key_value = project_key_value(inputs, low_rows, first_vec)
        query = project_query(inputs, low_rows, first_vec)
        pieces = [key_value, swap(key_value, "core", nc, 1)]
        offset = 1
        while offset < half:
            sent = jnp.concatenate(pieces)
            got = swap(sent, "x", nx, offset)
            pieces = [pieces[0], jnp.concatenate([sent[count:], got])]
            offset *= 2
        own, other = pieces
    cotangent_near, cotangent_far = grad_mine, grad_far
    w_qkv = low_rows
    ends = jnp.cumsum(lax.dynamic_index_in_dim(lengths, side, 0, keepdims=False))

    def documents(offset_x, offset_core):
        at = lax.broadcasted_iota(jnp.int32, (2, span), 1)
        part = lax.broadcasted_iota(jnp.int32, (2, span), 0)
        x_at = x_place ^ offset_x ^ (part * half)
        at = ((x_at * nc) + (core ^ offset_core)) * span + at
        at = at.reshape(-1, 1)
        return jnp.sum((at >= ends[None, :]).astype(jnp.int32), axis=-1, keepdims=True)

    slot = lax.broadcasted_iota(jnp.int32, (1, LANES), 1) % HEAD
    group = [(dx, dc) for dx in range(half) for dc in range(nc)]
    seg = [documents(dx, dc) for dx, dc in group]
    mask_q = jnp.where(slot == seg[0], -1e30, 0.0).astype(BF16)
    mask_own = (slot != seg[0]).astype(BF16)
    mask_other = (slot != jnp.concatenate(seg[1:])).astype(BF16)

    width = PAIRS // 2
    forward = []
    for part in range(2):
        forward.append(
            attend_forward(
                query, own, other, mask_q, mask_own, mask_other, part * width, width
            )
        )
    mixed = jnp.concatenate([forward[0][0], forward[1][0]], axis=1)
    if sizes == (4, 2, 2, 2):
        mixed, store, cotangent_far = fence((mixed, store, cotangent_far))

    biases = vectors_of(store)
    high_rows = store[-2]
    w_out = high_rows[:D]
    w_first = high_rows[D : D + FF]
    w_second = high_rows[D + FF :]
    b_out = biases[2 * D : 3 * D]
    gain_one = biases[3 * D : 4 * D]
    shift_one = biases[4 * D : 5 * D]
    gain_two = biases[5 * D : 6 * D]
    shift_two = biases[6 * D : 7 * D]
    b_second = biases[7 * D : 8 * D]
    b_first = biases[8 * D :]

    inputs_wide = inputs.astype(F32)
    hidden = inputs_wide + dot_nt(mixed, w_out) + b_out
    normed, unit_one, rate_one = norm(hidden, gain_one, shift_one)
    normed_low = normed.astype(BF16)
    active, slope = gelu_layer(normed_low, high_rows, b_first.reshape(1, -1), D)
    hidden_two = normed + dot_nn(active, w_second) + b_second
    result, unit_two, rate_two = norm(hidden_two, gain_two, shift_two)
    result = result.astype(BF16)

    def rows_of(left, right):
        return dot_tn(left, right).astype(BF16)

    def attend_back(part, d_mixed):
        return attend_backward(
            forward[part][1],
            forward[part][2],
            query,
            own,
            other,
            forward[part][0],
            d_mixed,
            part * width,
            width,
        )

    def feed_back(d_feed):
        d_inner = (dot_nt(d_feed, w_second) * slope.astype(F32)).astype(BF16)
        return d_inner, jnp.sum(d_inner.astype(F32), axis=0)

    def hidden_back(d_inner, d_hidden_two):
        d_normed = d_hidden_two + dot_nn(d_inner, w_first)
        d_hidden, d_gain, d_shift = norm_back(d_normed, unit_one, rate_one, gain_one)
        d_branch = d_hidden.astype(BF16)
        d_bias = jnp.sum(d_branch.astype(F32), axis=0)
        return d_hidden, d_branch, dot_nn(d_branch, w_out).astype(BF16), d_bias, d_gain, d_shift

    cotangent = jnp.concatenate([cotangent_near, cotangent_far]).astype(F32)
    d_hidden_two, d_gain_two, d_shift_two = norm_back(cotangent, unit_two, rate_two, gain_two)
    d_feed = d_hidden_two.astype(BF16)
    d_b_second = jnp.sum(d_feed.astype(F32), axis=0)

    if sizes == (4, 2, 2, 2):
        part_b = 2 * D

        def open_plane(*parts, vecs=None):
            block = parts[0] if len(parts) == 1 else jnp.concatenate(parts)
            return {"core": half_send(block.reshape(ny * nx, nc, share, D), 1, "core", vecs)}

        def first_send(plane, vecs=None):
            block = half_add(plane.pop("core"), 1, "core").reshape(ny, nx, share, D)
            plane["upper"] = half_send(block[:, :, :cut], 0, "y", vecs)
            plane["lower"] = half_send(block[:, :, cut:], 1, "x")

        def second_send(plane, vecs=None):
            plane["upper"] = half_send(half_add(plane["upper"], 0, "y"), 0, "x", vecs)
            plane["lower"] = half_send(half_add(plane["lower"], 1, "x"), 0, "y")

        def close(plane):
            return jnp.concatenate(
                [half_add(plane["upper"], 0, "x"), half_add(plane["lower"], 0, "y")]
            )

        live = {"third": rows_of(active[:, D:], d_feed), "d_feed": d_feed, "result": result}
        live = fence(live)

        p3 = open_plane(live.pop("third"))
        live["far"] = far(live["result"][span:])
        d_inner, d_b_first = feed_back(live["d_feed"])
        low_part = rows_of(active[:, :D], live["d_feed"])
        high_part = rows_of(d_inner[:, part_b:], normed_low)
        live |= {"p3": p3, "d_inner": d_inner, "low": low_part, "high": high_part}
        live["d_hidden_two"] = d_hidden_two
        live = fence(live)

        block_out = ungroup(live["result"][:span], live.pop("far"))
        first_send(live["p3"])
        live["p2"] = open_plane(live.pop("high"), live.pop("low"))
        d_hidden, d_branch, d_mixed, d_b_out, d_gain_one, d_shift_one = hidden_back(
            live["d_inner"], live["d_hidden_two"]
        )
        live |= {"d_hidden": d_hidden, "d_mixed": d_mixed}
        live["out_part"] = rows_of(d_branch, mixed)
        live["first_part"] = rows_of(live["d_inner"][:, :part_b], normed_low)
        live = fence(live)

        second_send(live["p3"])
        first_send(live["p2"])
        live["p1"] = open_plane(live.pop("out_part"), live.pop("first_part"))
        live["back_0"] = attend_back(0, live["d_mixed"])
        live = fence(live)

        live["closed_3"] = close(live.pop("p3"))
        second_send(live["p2"])
        first_send(live["p1"])
        live["kv_0"] = [swap(other_, "core", nc, 1) for other_ in live["back_0"][3:]]
        live["back_1"] = attend_back(1, live["d_mixed"])
        live = fence(live)

        live["closed_2"] = close(live.pop("p2"))
        second_send(live["p1"])
        live["kv_1"] = [swap(other_, "core", nc, 1) for other_ in live["back_1"][3:]]
        live = fence(live)

        live["closed_1"] = close(live.pop("p1"))
        columns = [[live[f"back_{h}"][0] for h in range(2)]]
        for n in range(2):
            columns.append(
                [add_low(live[f"back_{h}"][1 + n], live[f"kv_{h}"][n]) for h in range(2)]
            )
        d_query, _, d_value = (jnp.concatenate(c, axis=1) for c in columns)
        d_projected = jnp.concatenate([part for c in columns for part in c], axis=1)
        live["d_w_qkv"] = rows_of(d_projected, inputs)
        live["d_projected"] = d_projected
        live["d_query"], live["d_value"] = d_query, d_value
        for name in ("back_0", "back_1", "kv_0", "kv_1"):
            del live[name]
        live = fence(live)

        grad_vecs = [
            jnp.sum(live["d_query"].astype(F32), axis=0),
            jnp.sum(live["d_value"].astype(F32), axis=0),
            d_b_out,
            d_gain_one,
            d_shift_one,
            d_gain_two,
            d_shift_two,
            d_b_second,
            d_b_first,
        ]
        vecs = jnp.concatenate(grad_vecs).reshape(-1, D).astype(BF16)
        live["vecs"] = jnp.pad(vecs, ((0, 16 - vecs.shape[0]), (0, 0)))
        live["p0"] = open_plane(live.pop("d_w_qkv"), vecs=live["vecs"])
        live["d_inputs"] = live["d_hidden"] + dot_nn(live["d_projected"], w_qkv)
        live = fence(live)

        vecs = add_low(live["vecs"], live["p0"]["core"].pop("whole"))
        first_send(live["p0"], vecs)
        live["vecs"] = vecs
        sums = [None, live["closed_1"], live["closed_2"], live["closed_3"]]
        sent = jnp.where(z_place == 0, sums[3], jnp.where(z_place == 2, sums[1], sums[2]))
        live["z_got"] = swap(sent, "z", 4, 1)
        live = fence(live)

        vecs = add_low(live["vecs"], live["p0"]["upper"].pop("whole"))
        sums = [None, live["closed_1"], live["closed_2"], live["closed_3"]]
        second_send(live["p0"], vecs)
        live["vecs"] = vecs
        live["even_two"] = add_low(sums[2], live["z_got"])
        sent = add_low(jnp.where(z_place == 1, sums[3], sums[1]), live.pop("z_got"))
        live["z_got"] = lax.ppermute(sent, "z", [(1, 3), (3, 1)])
        live["away"] = far(live["d_inputs"][span:].astype(BF16))
        live = fence(live)

        vecs = add_low(live["vecs"], live["p0"]["upper"].pop("whole"))
        sums = [close(live.pop("p0")), live["closed_1"], live["closed_2"], live["closed_3"]]
        live["odd"] = add_low(jnp.where(z_place == 1, sums[1], sums[3]), live.pop("z_got"))
        sent = jnp.where(odd, sums[0], jnp.where(z_place == 0, sums[1], sums[3]))
        live["z_got"] = swap(jnp.concatenate([sent, vecs]), "z", 4, 1)
        live["zero"], live["vecs"] = sums[0], vecs
        live = fence(live)

        vecs = add_low(live["vecs"], live["z_got"][share:])
        z_got = live.pop("z_got")[:share]
        odd_own = live["odd"].astype(F32) + z_got.astype(F32)
        even_zero = add_low(live["zero"], z_got)
        even_two = live["even_two"]
        live["z_got"] = lax.ppermute(
            jnp.where(z_place == 0, even_two, even_zero), "z", [(0, 2), (2, 0)]
        )
        live["vecs"] = {"all": vecs, "got": swap(vecs, "z", 4, 2)}
        input_grad = ungroup(live["d_inputs"][:span], live.pop("away").astype(F32))
        live["kept"] = jnp.where(z_place == 0, even_zero, even_two)
        live["odd"] = odd_own
        live = fence(live)

        vecs = live["vecs"]["all"].astype(F32) + live["vecs"]["got"].astype(F32)
        owner = ((z_place * ny + lax.axis_index("y")) * nx + x_place) * nc + core
        own_vecs = lax.dynamic_slice(vecs.reshape(-1), (owner * share,), (share,))
        even_own = live["kept"].astype(F32) + live["z_got"].astype(F32)
        own_mats = jnp.where(odd, live["odd"], even_own)
    else:
        block_out = ungroup(result[:span], far(result[span:]))
        d_w_second = rows_of(active, d_feed)
        d_inner, d_b_first = feed_back(d_feed)
        d_w_first = rows_of(d_inner, normed_low)
        d_hidden, d_branch, d_mixed, d_b_out, d_gain_one, d_shift_one = hidden_back(
            d_inner, d_hidden_two
        )
        d_w_out = rows_of(d_branch, mixed)

        def send_back(mine, others):
            offset = half // 2
            while offset >= 1:
                rows = offset * nc * count
                got = swap(others[rows - count :], "x", nx, offset)
                mine = add_low(mine, got[:count])
                others = add_low(others[: rows - count], got[count:])
                offset //= 2
            return add_low(mine, swap(others, "core", nc, 1))

        columns = [[], [], []]
        for part in range(2):
            d_query, d_key_own, d_value_own, d_key_other, d_value_other = attend_back(
                part, d_mixed
            )
            columns[0].append(d_query)
            columns[1].append(send_back(d_key_own, d_key_other))
            columns[2].append(send_back(d_value_own, d_value_other))
        d_query, _, d_value = (jnp.concatenate(c, axis=1) for c in columns)
        d_projected = jnp.concatenate([part for c in columns for part in c], axis=1)
        d_w_qkv = rows_of(d_projected, inputs)
        d_inputs = d_hidden + dot_nn(d_projected, w_qkv)
        d_away = far(d_inputs[span:].astype(BF16)).astype(F32)
        input_grad = ungroup(d_inputs[:span], d_away)
        grad_rows = jnp.concatenate([d_w_qkv, d_w_out, d_w_first, d_w_second])
        own_mats = jnp.zeros((share, D), F32)
        for plane in range(nz):
            block = grad_rows[plane * plane_rows : (plane + 1) * plane_rows]
            block = fold(block.reshape(ny * nx, nc, share, D), 1, "core", nc, add_low)
            block = fold(block.reshape(ny, nx, share, D), 0, "y", ny, add_low)
            block = fold(block, 1, "x", nx, add_low).reshape(share, D)
            block = reduce_plane(block, plane, nz)
            own_mats = jnp.where(z_place == plane, block.astype(F32), own_mats)
        grad_vecs = jnp.concatenate(
            [
                jnp.sum(d_query.astype(F32), axis=0),
                jnp.sum(d_value.astype(F32), axis=0),
                d_b_out,
                d_gain_one,
                d_shift_one,
                d_gain_two,
                d_shift_two,
                d_b_second,
                d_b_first,
            ]
        )
        for axis, size in (("z", nz), ("y", ny), ("x", nx), ("core", nc)):
            grad_vecs = fold(grad_vecs, 0, axis, size, jnp.add)
        own_vecs = grad_vecs

    new_mats, first_mats, later_mats = adamw(
        mats, own_mats.T, moment_mats, second_mats, rate_mats, weight_decay
    )
    new_vecs, first_vecs, later_vecs = adamw(
        vectors, own_vecs, moment_vecs, second_vecs, rate_vecs, 0.0
    )
    return (
        block_out,
        input_grad,
        new_mats,
        first_mats,
        later_mats,
        new_vecs,
        first_vecs,
        later_vecs,
    )


def solution(mesh):
    dp, seq = mesh.shape["dp"], mesh.shape["seq"]
    ny = 2 ** ((dp.bit_length() - 1) // 2)
    sizes = (dp // ny, ny, seq // 2, 2)
    fine = Mesh(mesh.devices.reshape(sizes), ("z", "y", "x", "core"))
    rows, every = ("z", "y"), ("z", "y", "x", "core")
    tokens = P(rows, ("x", "core"), None)
    return jax.shard_map(
        functools.partial(local, sizes),
        mesh=fine,
        in_specs=(
            tokens,
            P(rows, None),
            tokens,
            P(None, every),
            P(every),
            P(None, every),
            P(None, every),
            P(every),
            P(every),
        ),
        out_specs=(
            tokens,
            tokens,
            P(None, every),
            P(None, every),
            P(None, every),
            P(every),
            P(every),
            P(every),
        ),
        check_vma=False,
    )
```

```python
import functools

import jax
import jax.numpy as jnp
from jax import lax
from jax.experimental import pallas as pl
from jax.experimental.pallas import tpu as pltpu
from jax.sharding import Mesh
from jax.sharding import PartitionSpec as P

D = 768
HEADS = 12
HEAD = D // HEADS
FF = 3072
STEP = 10
LANES = 128
PAIRS = D // LANES


norm_eps = 1e-05
first_decay = 0.9
second_decay = 0.999
adam_eps = 1e-08
rate_mats = 0.08
rate_vecs = 0.4
weight_decay = 0.01

F32 = jnp.float32
QUICK = pl.CostEstimate(flops=0, bytes_accessed=0, transcendentals=0)
BF16 = jnp.bfloat16


def dot_nn(left, right):
    return lax.dot_general(left, right, (((1,), (0,)), ((), ())), preferred_element_type=F32)


def dot_nt(left, right):
    return lax.dot_general(left, right, (((1,), (1,)), ((), ())), preferred_element_type=F32)


def dot_tn(left, right):
    return lax.dot_general(left, right, (((0,), (0,)), ((), ())), preferred_element_type=F32)


def adamw(weight, gradient, moment, second, rate, decay):
    moment_new = first_decay * moment + (1.0 - first_decay) * gradient
    second_new = second_decay * second + (1.0 - second_decay) * gradient * gradient
    fixed_first = moment_new / (1.0 - first_decay**STEP)
    fixed_second = second_new / (1.0 - second_decay**STEP)
    weight_new = weight - rate * (
        fixed_first / (jnp.sqrt(fixed_second) + adam_eps) + decay * weight
    )
    return (weight_new, moment_new, second_new)


def attend_forward_kernel(
    q_ref, ko_ref, vo_ref, kt_ref, vt_ref, mq_ref, mo_ref, mt_ref, a_ref, e_ref, inv_ref
):
    count = q_ref.shape[0]
    own = ko_ref.shape[0]
    total = own + kt_ref.shape[0]
    q = q_ref[...]
    lane = lax.broadcasted_iota(jnp.int32, (1, LANES), 1)
    row = lax.broadcasted_iota(jnp.int32, (LANES, 1), 0)
    value_t = jnp.concatenate([vo_ref[...].T, vt_ref[...].T], axis=1)
    halves = []
    for h in range(2):
        inside = (lane < HEAD) if h == 0 else (lane >= HEAD)
        inside_row = (row < HEAD) if h == 0 else (row >= HEAD)
        q_h = jnp.where(inside, q, mq_ref[...])
        k_o = jnp.where(inside, ko_ref[...], mo_ref[...])
        k_t = jnp.where(inside, kt_ref[...], mt_ref[...])
        s_o = dot_nt(k_o, q_h)
        s_t = dot_nt(k_t, q_h)
        top = jnp.maximum(
            jnp.max(s_o, axis=0, keepdims=True), jnp.max(s_t, axis=0, keepdims=True)
        )
        e_ref[h, 0:own, :] = jnp.exp(s_o - top).astype(BF16)
        e_ref[h, own:total, :] = jnp.exp(s_t - top).astype(BF16)
        v_h = jnp.where(inside_row, value_t, jnp.ones_like(value_t))
        mixed = dot_nn(v_h, e_ref[h])
        one = HEAD if h == 0 else 0
        inverse = 1.0 / mixed[one : one + 1, :]
        inv_ref[0, h : h + 1, :] = inverse
        halves.append(mixed * inverse)
    both = jnp.where(row < HEAD, halves[0], halves[1])
    a_ref[...] = both.T.astype(BF16)


def attend_forward(q, own, other, mask_q, mask_own, mask_other, first, pairs):
    count = q.shape[0]
    here, there = own.shape[0], other.shape[0]
    place = lambda j: (0, j)
    column = lambda j: (0, j + first)
    shifted = lambda j: (0, j + first + PAIRS)
    whole = lambda j: (0, 0)
    return pl.pallas_call(
        attend_forward_kernel,
        grid=(pairs,),
        in_specs=[
            pl.BlockSpec((count, LANES), column),
            pl.BlockSpec((here, LANES), column),
            pl.BlockSpec((here, LANES), shifted),
            pl.BlockSpec((there, LANES), column),
            pl.BlockSpec((there, LANES), shifted),
            pl.BlockSpec((count, LANES), whole),
            pl.BlockSpec((here, LANES), whole),
            pl.BlockSpec((there, LANES), whole),
        ],
        out_specs=[
            pl.BlockSpec((count, LANES), place),
            pl.BlockSpec((2, here + there, count), lambda j: (j, 0, 0)),
            pl.BlockSpec((1, 2, count), lambda j: (j, 0, 0)),
        ],
        out_shape=[
            jax.ShapeDtypeStruct((count, pairs * LANES), BF16),
            pltpu.HBM((2 * pairs, here + there, count), BF16),
            jax.ShapeDtypeStruct((pairs, 2, count), F32),
        ],
        compiler_params=pltpu.CompilerParams(vmem_limit_bytes=52 * 2**20),
        cost_estimate=QUICK,
        name="attend_forward",
    )(q, own, own, other, other, mask_q, mask_own, mask_other)


def attend_backward_kernel(
    e_ref,
    inv_ref,
    q_ref,
    ko_ref,
    vo_ref,
    kt_ref,
    vt_ref,
    a_ref,
    da_ref,
    dq_ref,
    dko_ref,
    dvo_ref,
    dkt_ref,
    dvt_ref,
    ds_ref,
):
    own = ko_ref.shape[0]
    total = own + kt_ref.shape[0]
    lane = lax.broadcasted_iota(jnp.int32, (1, LANES), 1)
    row = lax.broadcasted_iota(jnp.int32, (LANES, 1), 0)
    da = da_ref[...]
    zero = jnp.zeros_like(da)
    product = (da.astype(F32) * a_ref[...].astype(F32)).T
    inv_t = jnp.where(row < HEAD, inv_ref[0, 0:1, :], inv_ref[0, 1:2, :])
    inverse = inv_t.T
    da_scaled = (da.astype(F32) * inverse).astype(BF16)
    q_scaled = (q_ref[...].astype(F32) * inverse).astype(BF16)
    keys_t = jnp.concatenate([ko_ref[...].T, kt_ref[...].T], axis=1)
    d_value = None
    d_key = None
    halves = []
    for h in range(2):
        inside = (lane < HEAD) if h == 0 else (lane >= HEAD)
        da_h = jnp.where(inside, da, zero)
        delta = jnp.sum(product[h * HEAD : (h + 1) * HEAD, :], axis=0, keepdims=True)
        dp_o = dot_nt(vo_ref[...], da_h)
        ds_ref[h, 0:own, :] = (e_ref[h, 0:own, :].astype(F32) * (dp_o - delta)).astype(BF16)
        dp_t = dot_nt(vt_ref[...], da_h)
        ds_ref[h, own:total, :] = (
            e_ref[h, own:total, :].astype(F32) * (dp_t - delta)
        ).astype(BF16)
        part_v = dot_nn(e_ref[h], jnp.where(inside, da_scaled, zero))
        part_k = dot_nn(ds_ref[h], jnp.where(inside, q_scaled, zero))
        d_value = part_v if d_value is None else d_value + part_v
        d_key = part_k if d_key is None else d_key + part_k
        halves.append(dot_nn(keys_t, ds_ref[h]))
    both = jnp.where(row < HEAD, halves[0], halves[1]) * inv_t
    dq_ref[...] = (both.T * (HEAD**-0.5)).astype(BF16)
    dko_ref[...] = d_key[0:own].astype(BF16)
    dvo_ref[...] = d_value[0:own].astype(BF16)
    dkt_ref[...] = d_key[own:total].astype(BF16)
    dvt_ref[...] = d_value[own:total].astype(BF16)


def attend_backward(e, inverse, q, own, other, a, da, first, pairs):
    count = q.shape[0]
    here, there = own.shape[0], other.shape[0]
    place = lambda j: (0, j)
    column = lambda j: (0, j + first)
    shifted = lambda j: (0, j + first + PAIRS)
    mine = pl.BlockSpec((count, LANES), column)
    width = pairs * LANES
    return pl.pallas_call(
        attend_backward_kernel,
        grid=(pairs,),
        in_specs=[
            pl.BlockSpec((2, here + there, count), lambda j: (j, 0, 0)),
            pl.BlockSpec((1, 2, count), lambda j: (j, 0, 0)),
            mine,
            pl.BlockSpec((here, LANES), column),
            pl.BlockSpec((here, LANES), shifted),
            pl.BlockSpec((there, LANES), column),
            pl.BlockSpec((there, LANES), shifted),
            pl.BlockSpec((count, LANES), place),
            mine,
        ],
        out_specs=[
            pl.BlockSpec((count, LANES), place),
            pl.BlockSpec((here, LANES), place),
            pl.BlockSpec((here, LANES), place),
            pl.BlockSpec((there, LANES), place),
            pl.BlockSpec((there, LANES), place),
        ],
        out_shape=[
            jax.ShapeDtypeStruct((count, width), BF16),
            jax.ShapeDtypeStruct((here, width), BF16),
            jax.ShapeDtypeStruct((here, width), BF16),
            jax.ShapeDtypeStruct((there, width), BF16),
            jax.ShapeDtypeStruct((there, width), BF16),
        ],
        scratch_shapes=[pltpu.VMEM((2, here + there, count), BF16)],
        compiler_params=pltpu.CompilerParams(vmem_limit_bytes=52 * 2**20),
        cost_estimate=QUICK,
        name="attend_backward",
    )(e, inverse, q, own, own, other, other, a, da)


def feed_kernel(y_ref, first_ref, second_ref, b_ref, u_ref, slope_ref, f_ref):
    z = dot_nt(y_ref[...], first_ref[...]) + b_ref[...]
    cdf = 0.5 + 0.5 * lax.erf(z * (0.5**0.5))
    density = jnp.exp(-0.5 * z * z) * 0.3989422804014327
    u = (z * cdf).astype(BF16)
    u_ref[...] = u
    slope_ref[...] = (cdf + z * density).astype(BF16)
    part = dot_nn(u, second_ref[...])

    @pl.when(pl.program_id(0) == 0)
    def _():
        f_ref[...] = part

    @pl.when(pl.program_id(0) > 0)
    def _():
        f_ref[...] += part


def feed_layer(y, rows, b, first, block=512):
    count = y.shape[0]
    whole = pl.BlockSpec((count, D), lambda j: (0, 0))
    column = pl.BlockSpec((count, block), lambda j: (0, j))
    begin = first // block
    return pl.pallas_call(
        feed_kernel,
        grid=(FF // block,),
        in_specs=[
            whole,
            pl.BlockSpec((block, D), lambda j: (j + begin, 0)),
            pl.BlockSpec((block, D), lambda j: (j + begin + FF // block, 0)),
            pl.BlockSpec((1, block), lambda j: (0, j)),
        ],
        out_specs=[column, column, whole],
        out_shape=[
            jax.ShapeDtypeStruct((count, FF), BF16),
            jax.ShapeDtypeStruct((count, FF), BF16),
            jax.ShapeDtypeStruct((count, D), F32),
        ],
        compiler_params=pltpu.CompilerParams(vmem_limit_bytes=30 * 2**20),
        cost_estimate=QUICK,
        name="feed_layer",
    )(y, rows, rows, b)


def project_kernel(x_ref, w_ref, b_ref, q_ref, kv_ref):
    value = (dot_nt(x_ref[...], w_ref[...]) + b_ref[...]).astype(BF16)
    step = pl.program_id(0)

    @pl.when(step == 0)
    def _():
        q_ref[...] = (value.astype(F32) * HEAD**-0.5).astype(BF16)

    @pl.when(step > 0)
    def _():
        kv_ref[...] = value


def project(inputs, rows, bias):
    count = inputs.shape[0]
    return pl.pallas_call(
        project_kernel,
        grid=(3,),
        in_specs=[
            pl.BlockSpec((count, D), lambda j: (0, 0)),
            pl.BlockSpec((D, D), lambda j: (j, 0)),
            pl.BlockSpec((1, D), lambda j: (0, j)),
        ],
        out_specs=[
            pl.BlockSpec((count, D), lambda j: (0, 0)),
            pl.BlockSpec((count, D), lambda j: (0, jnp.maximum(j - 1, 0))),
        ],
        out_shape=[
            jax.ShapeDtypeStruct((count, D), BF16),
            jax.ShapeDtypeStruct((count, 2 * D), BF16),
        ],
        compiler_params=pltpu.CompilerParams(vmem_limit_bytes=32 * 2**20),
        cost_estimate=QUICK,
        name="project",
    )(inputs, rows, bias)


def feed_back_kernel(
    df_ref, y_ref, second_ref, first_ref, u_ref, slope_ref, low_ref, high_ref, dfirst_ref, dy_ref, db_ref
):
    step = pl.program_id(0)
    df = df_ref[...]
    dsecond = dot_tn(u_ref[...], df).astype(BF16)

    @pl.when(step == 0)
    def _():
        low_ref[...] = dsecond

    @pl.when(step > 0)
    def _():
        high_ref[...] = dsecond

    dz = (dot_nt(df, second_ref[...]) * slope_ref[...].astype(F32)).astype(BF16)
    db_ref[...] = jnp.sum(dz.astype(F32), axis=0, keepdims=True)
    dfirst_ref[...] = dot_tn(dz, y_ref[...]).astype(BF16)
    part = dot_nn(dz, first_ref[...])

    @pl.when(step == 0)
    def _():
        dy_ref[...] = part

    @pl.when(step > 0)
    def _():
        dy_ref[...] += part


def feed_back_layer(df, y, rows, first, u, slope):
    count = df.shape[0]
    whole = pl.BlockSpec((count, D), lambda j: (0, 0))
    column = pl.BlockSpec((count, D), lambda j: (0, j))
    begin = first // D
    return pl.pallas_call(
        feed_back_kernel,
        grid=(FF // D,),
        in_specs=[
            whole,
            whole,
            pl.BlockSpec((D, D), lambda j: (j + begin + FF // D, 0)),
            pl.BlockSpec((D, D), lambda j: (j + begin, 0)),
            column,
            column,
        ],
        out_specs=[
            pl.BlockSpec((D, D), lambda j: (0, 0)),
            pl.BlockSpec((D, D), lambda j: (jnp.maximum(j - 1, 0), 0)),
            pl.BlockSpec((D, D), lambda j: (j, 0)),
            whole,
            pl.BlockSpec((1, D), lambda j: (0, j)),
        ],
        out_shape=[
            jax.ShapeDtypeStruct((D, D), BF16),
            jax.ShapeDtypeStruct((FF - D, D), BF16),
            jax.ShapeDtypeStruct((FF, D), BF16),
            jax.ShapeDtypeStruct((count, D), F32),
            jax.ShapeDtypeStruct((1, FF), F32),
        ],
        compiler_params=pltpu.CompilerParams(vmem_limit_bytes=32 * 2**20),
        cost_estimate=QUICK,
        name="feed_back",
    )(df, y, rows, rows, u, slope)


def pack_kernel(width, *refs):
    *sources, out_ref = refs
    sums = [jnp.sum(ref[...].astype(F32), axis=0, keepdims=True) for ref in sources[:6]]
    out_ref[...] = jnp.zeros_like(out_ref)
    out_ref[0:1, :width] = sums[0].astype(BF16)
    out_ref[0:1, width:] = sums[1].astype(BF16)
    out_ref[1:2, :width] = (sums[2] + sums[3]).astype(BF16)
    out_ref[1:2, width:] = (sums[4] + sums[5]).astype(BF16)
    row = 2
    for ref in sources[6:]:
        for part in range(ref.shape[1] // D):
            out_ref[row : row + 1, :] = ref[:, part * D : (part + 1) * D].astype(BF16)
            row += 1


def pack_vectors(backs, others):
    (q_0, _, v_0, _, far_0), (q_1, _, v_1, _, far_1) = backs
    others = [other.reshape(1, -1) for other in others]
    return pl.pallas_call(
        functools.partial(pack_kernel, q_0.shape[1]),
        out_shape=jax.ShapeDtypeStruct((16, D), BF16),
        compiler_params=pltpu.CompilerParams(vmem_limit_bytes=32 * 2**20),
        cost_estimate=QUICK,
        name="pack_vectors",
    )(q_0, q_1, v_0, far_0, v_1, far_1, *others)


def partners(size, offset):
    return [(i, i ^ offset) for i in range(size)]


def swap(value, axis, size, offset):
    return lax.ppermute(value, axis, partners(size, offset))


def add_low(left, right):
    return (left.astype(F32) + right.astype(F32)).astype(BF16)


def assemble(found, share, sizes):
    ny, nx, nc = sizes
    owners = ny * nx * nc

    def target(offset):
        dy, dx, dc = offset
        y = lax.axis_index("y") ^ dy
        x = lax.axis_index("x") ^ dx
        core = lax.axis_index("core") ^ dc
        return (y * nx + x) * nc + core

    arrays = []
    for array, *_ in found:
        if not any(array is other for other in arrays):
            arrays.append(array)
    places = [next(i for i, o in enumerate(arrays) if o is f[0]) for f in found]

    def kernel(*refs):
        sources = refs[: len(arrays)]
        out, out_vec, sems, sems_vec = refs[len(arrays) :]
        copies = []
        for n, (array, k, offset, first) in enumerate(found):
            count = min(array.shape[1], share - first)
            source = sources[places[n]]
            start = pl.multiple_of(target(offset) * share + first, 16)
            copies.append(
                pltpu.make_async_copy(
                    source.at[k, pl.ds(0, count), :], out.at[pl.ds(start, count), :], sems.at[n]
                )
            )
            if count < array.shape[1]:
                start = pl.multiple_of(target(offset) * 16, 16)
                copies.append(
                    pltpu.make_async_copy(
                        source.at[k, pl.ds(count, 16), :],
                        out_vec.at[pl.ds(start, 16), :],
                        sems_vec.at[n],
                    )
                )
        for copy in copies:
            copy.start()
        for copy in copies:
            copy.wait()

    inside = pl.BlockSpec(memory_space=pltpu.VMEM)
    return pl.pallas_call(
        kernel,
        in_specs=[pl.BlockSpec(memory_space=pl.ANY)] * len(arrays),
        out_specs=[inside] * 2,
        out_shape=[
            jax.ShapeDtypeStruct((owners * share, D), BF16),
            jax.ShapeDtypeStruct((owners * 16, D), BF16),
        ],
        scratch_shapes=[
            pltpu.SemaphoreType.DMA((len(found),)),
            pltpu.SemaphoreType.DMA((len(found),)),
        ],
        compiler_params=pltpu.CompilerParams(vmem_limit_bytes=16 * 2**20),
        cost_estimate=QUICK,
        name="assemble",
    )(*arrays)


class Pull:
    def __init__(self, bag):
        self.bag = bag

    def __getattr__(self, name):
        return self.bag.pop(name)


class Bag(dict):
    __setattr__ = dict.__setitem__
    __delattr__ = dict.__delitem__
    pull = property(Pull)

    def __getattr__(self, name):
        return self[name]


def plain(value):
    return {k: plain(v) for k, v in value.items()} if isinstance(value, dict) else value


def bagged(value):
    return Bag({k: bagged(v) for k, v in value.items()}) if isinstance(value, dict) else value


def fence(live):
    return bagged(lax.optimization_barrier(plain(live)))


def plane_start(block, cut):
    return Bag(parts=[block[None, :cut], block[None, cut:]])


def plane_first(plane):
    upper, lower = plane.parts
    plane.got = [swap(upper, "x", 2, 1), swap(lower, "y", 2, 1)]


def plane_second(plane):
    pairs = [jnp.concatenate(both) for both in zip(plane.pull.parts, plane.pull.got)]
    plane.own = pairs + [swap(pairs[0], "y", 2, 1), swap(pairs[1], "x", 2, 1)]


def plane_cores(plane):
    plane.other = [swap(array, "core", 2, 1) for array in plane.own]


def plane_found(plane, cut):
    places = [((0, 0), (0, 1)), ((0, 0), (1, 0)), ((1, 0), (1, 1)), ((0, 1), (1, 1))]
    found = []
    for core, arrays in enumerate((plane.own, plane.other)):
        for n, (array, offsets) in enumerate(zip(arrays, places)):
            for k, offset in enumerate(offsets):
                found.append((array, k, (*offset, core), 0 if n % 2 == 0 else cut))
    return found


def take(value, index, dim):
    return lax.dynamic_index_in_dim(value, index, dim, keepdims=False)


def half_send(value, dim, axis, whole=None):
    place = lax.axis_index(axis)
    away = take(value, 1 - place, dim)
    if whole is None:
        return Bag(all=value, got=swap(away, axis, 2, 1))
    rows = jnp.concatenate([away.reshape(-1, D), whole])
    got = swap(rows, axis, 2, 1)
    return Bag(all=value, got=got[:-16].reshape(away.shape), whole=got[-16:])


def half_add(sent, dim, axis):
    return add_low(take(sent.all, lax.axis_index(axis), dim), sent.got)


def norm(values, gain, shift):
    center = values - jnp.mean(values, axis=-1, keepdims=True)
    spread_ = jnp.mean(center * center, axis=-1, keepdims=True)
    rate = lax.rsqrt(spread_ + norm_eps)
    unit = center * rate
    return unit * gain + shift, unit, rate


def norm_back(cotangent, unit, rate, gain):
    scaled = cotangent * gain
    mean = jnp.mean(scaled, axis=-1, keepdims=True)
    along = jnp.mean(scaled * unit, axis=-1, keepdims=True)
    grad = rate * (scaled - mean - unit * along)
    return grad, jnp.sum(cotangent * unit, axis=0), jnp.sum(cotangent, axis=0)


def local(
    sizes,
    tokens,
    lengths,
    out_grad,
    mats,
    vectors,
    moment_mats,
    second_mats,
    moment_vecs,
    second_vecs,
):
    nz, ny, nx, nc = sizes
    flat = (ny, nx, nc)
    sequences, span, _ = tokens.shape
    share = mats.shape[1]
    cut = share // 2 // 16 * 16
    x_place, core = lax.axis_index("x"), lax.axis_index("core")
    half = nx // 2
    side = x_place // half

    def regroup(value):
        mine = lax.dynamic_index_in_dim(value, side, 0, keepdims=False)
        away = lax.dynamic_index_in_dim(value, 1 - side, 0, keepdims=False)
        return mine, away

    def far(value):
        return swap(value, "x", nx, half)

    def ungroup(mine, got):
        low, high = (jnp.stack([mine, got]), jnp.stack([got, mine]))
        return jnp.where(side == 0, low, high)

    count = sequences * span

    ends = jnp.cumsum(lax.dynamic_index_in_dim(lengths, side, 0, keepdims=False))

    def documents(offset_x, offset_core):
        at = lax.broadcasted_iota(jnp.int32, (2, span), 1)
        part = lax.broadcasted_iota(jnp.int32, (2, span), 0)
        x_at = x_place ^ offset_x ^ (part * half)
        at = ((x_at * nc) + (core ^ offset_core)) * span + at
        at = at.reshape(-1, 1)
        return jnp.sum((at >= ends[None, :]).astype(jnp.int32), axis=-1, keepdims=True)

    slot = lax.broadcasted_iota(jnp.int32, (1, LANES), 1) % HEAD
    group = [(dx, dc) for dx in range(half) for dc in range(nc)]
    seg = [documents(dx, dc) for dx, dc in group]
    mask_q = jnp.where(slot == seg[0], -1e30, 0.0).astype(BF16)
    mask_own = (slot != seg[0]).astype(BF16)
    mask_other = (slot != jnp.concatenate(seg[1:])).astype(BF16)
    width = PAIRS // 2

    def attend(part, query, own, other):
        return attend_forward(
            query, own, other, mask_q, mask_own, mask_other, part * width, width
        )

    every = ("z", "y", "x", "core")
    shard = mats.T.astype(BF16)
    rows = lax.all_gather(shard, every, axis=0, tiled=True)
    token_mine, token_away = regroup(tokens)
    grad_mine, grad_away = regroup(out_grad)

    def project_all(inputs, rows, vec):
        bias = jnp.concatenate([vec[:D], jnp.zeros((D,), F32), vec[D : 2 * D]])
        return project(inputs, rows, bias.reshape(1, -1))

    z_place, y_place = lax.axis_index("z"), lax.axis_index("y")
    if sizes == (4, 2, 2, 2):
        odd = z_place % 2 == 1
        vec = jnp.pad(vectors, (0, D - share)).reshape(1, D).astype(BF16)
        at = lax.broadcasted_iota(jnp.int32, (16, D), 0)
        vec = jnp.where(at == z_place, vec, jnp.zeros_like(vec))

        live = Bag(shard=shard, vec=vec)
        live.got = lax.ppermute(shard, "z", [(0, 2)])
        live.vec_got = swap(vec, "z", 4, 2)
        live.token_far = far(token_away)
        live = fence(live)

        live.shard = jnp.where(z_place == 2, live.got, live.shard)
        live.vec = live.vec + live.vec_got
        live.got = lax.ppermute(live.shard, "z", [(0, 1), (2, 3)])
        live.vec_got = swap(live.vec, "z", 4, 1)
        live = fence(live)

        block = jnp.where(odd, live.pull.got, live.pull.shard)
        live.plane = plane_start(
            jnp.concatenate([block, live.pull.vec + live.pull.vec_got]), cut
        )
        plane_first(live.plane)
        plane_second(live.plane)
        live = fence(live)

        plane_cores(live.plane)
        live.inputs = jnp.concatenate([token_mine, live.pull.token_far])
        live = fence(live)

        w_qkv, vecs = assemble(plane_found(live.pull.plane, cut), share, flat)
        vecs = vecs.reshape(-1, 16, D)[:, :nz, :share]
        live.biases = vecs.transpose(1, 0, 2).reshape(-1).astype(F32)
        live.query, live.key_value = project_all(live.inputs, w_qkv, live.biases)
        live = fence(live)

        live.kv_got = swap(live.key_value, "core", nc, 1)
        live = fence(live)

        grad_far = far(grad_away)
        inputs, query, biases = live.inputs, live.query, live.biases
        own, other = live.key_value, live.kv_got
    else:
        token_far, grad_far = far(token_away), far(grad_away)
        biases = lax.all_gather(vectors.astype(BF16), every, axis=0, tiled=True).astype(F32)
        inputs = jnp.concatenate([token_mine, token_far])
        query, key_value = project_all(inputs, rows, biases)
        pieces = [key_value, swap(key_value, "core", nc, 1)]
        offset = 1
        while offset < half:
            sent = jnp.concatenate(pieces)
            got = swap(sent, "x", nx, offset)
            pieces = [pieces[0], jnp.concatenate([sent[count:], got])]
            offset *= 2
        own, other = pieces
    forward = [attend(part, query, own, other) for part in range(2)]
    mixed = jnp.concatenate([forward[0][0], forward[1][0]], axis=1)
    mixed, rows, grad_far = lax.optimization_barrier((mixed, rows, grad_far))
    cotangent_near, cotangent_far = grad_mine, grad_far
    w_qkv, w_out = rows[: 3 * D], rows[3 * D : 4 * D]
    first_row = 4 * D
    b_out = biases[2 * D : 3 * D]
    gain_one = biases[3 * D : 4 * D]
    shift_one = biases[4 * D : 5 * D]
    gain_two = biases[5 * D : 6 * D]
    shift_two = biases[6 * D : 7 * D]
    b_second = biases[7 * D : 8 * D]
    b_first = biases[8 * D :]

    inputs_wide = inputs.astype(F32)
    hidden = inputs_wide + dot_nt(mixed, w_out) + b_out
    normed, unit_one, rate_one = norm(hidden, gain_one, shift_one)
    normed_low = normed.astype(BF16)
    active, slope, feed = feed_layer(normed_low, rows, b_first.reshape(1, -1), first_row)
    hidden_two = normed + feed + b_second
    result, unit_two, rate_two = norm(hidden_two, gain_two, shift_two)
    result = result.astype(BF16)

    def total(rows):
        return jnp.sum(rows.astype(F32), axis=0)

    def rows_of(left, right):
        return dot_tn(left, right).astype(BF16)

    def attend_back(part, d_mixed):
        return attend_backward(
            forward[part][1],
            forward[part][2],
            query,
            own,
            other,
            forward[part][0],
            d_mixed,
            part * width,
            width,
        )

    def hidden_back(d_inner, d_hidden_two):
        d_normed = d_hidden_two + d_inner
        d_hidden, d_gain, d_shift = norm_back(d_normed, unit_one, rate_one, gain_one)
        d_branch = d_hidden.astype(BF16)
        d_bias = jnp.sum(d_branch.astype(F32), axis=0)
        return d_hidden, d_branch, dot_nn(d_branch, w_out).astype(BF16), d_bias, d_gain, d_shift

    cotangent = jnp.concatenate([cotangent_near, cotangent_far]).astype(F32)
    d_hidden_two, d_gain_two, d_shift_two = norm_back(cotangent, unit_two, rate_two, gain_two)
    d_feed = d_hidden_two.astype(BF16)
    d_b_second = jnp.sum(d_feed.astype(F32), axis=0)
    d_second_low, d_second_high, d_w_first, d_inner, d_b_first = feed_back_layer(
        d_feed, normed_low, rows, first_row, active, slope
    )
    d_b_first = d_b_first.reshape(-1)

    if sizes == (4, 2, 2, 2):
        def open_plane(block, vecs=None):
            return Bag(core=half_send(block.reshape(ny * nx, nc, share, D), 1, "core", vecs))

        def first_send(plane, vecs=None):
            block = half_add(plane.pull.core, 1, "core").reshape(ny, nx, share, D)
            plane.upper = half_send(block[:, :, :cut], 0, "y", vecs)
            plane.lower = half_send(block[:, :, cut:], 1, "x")

        def second_send(plane, vecs=None):
            plane.upper = half_send(half_add(plane.upper, 0, "y"), 0, "x", vecs)
            plane.lower = half_send(half_add(plane.lower, 1, "x"), 0, "y")

        def close(plane):
            return jnp.concatenate(
                [half_add(plane.upper, 0, "x"), half_add(plane.lower, 0, "y")]
            )

        live = Bag(third=d_second_high, d_w_first=d_w_first, low=d_second_low, result=result)
        live.update(d_inner=d_inner, d_hidden_two=d_hidden_two)
        live = fence(live)

        d_hidden, d_branch, d_mixed, d_b_out, d_gain_one, d_shift_one = hidden_back(
            live.pull.d_inner, live.pull.d_hidden_two
        )
        live.update(d_hidden=d_hidden, d_mixed=d_mixed)
        middle = [rows_of(d_branch, mixed), live.pull.d_w_first, live.pull.low]
        middle = jnp.concatenate(middle).reshape(2, ny * nx * nc, share, D)
        live.middle = middle.transpose(1, 0, 2, 3).reshape(-1, D)
        live = fence(live)

        middle = lax.psum_scatter(
            live.pull.middle, ("y", "x", "core"), scatter_dimension=0, tiled=True
        )
        live.p3 = open_plane(live.pull.third)
        live.far = far(live.result[span:])
        live.back_0 = attend_back(0, live.d_mixed)
        live = fence(live)

        block_out = ungroup(live.pull.result[:span], live.pull.far)
        first_send(live.p3)
        live.kv_0 = [swap(other_, "core", nc, 1) for other_ in live.back_0[3:]]
        live.back_1 = attend_back(1, live.d_mixed)
        live = fence(live)

        live.kv_1 = [swap(other_, "core", nc, 1) for other_ in live.back_1[3:]]
        others = [d_b_out, d_gain_one, d_shift_one, d_gain_two, d_shift_two, d_b_second, d_b_first]
        live.vecs = pack_vectors((live.back_0, live.back_1), others)
        live.vec_got = swap(live.vecs, "z", 4, 2)
        columns = [[back[0] for back in (live.back_0, live.back_1)]]
        for n in range(2):
            columns.append(
                [add_low(live.back_0[1 + n], live.kv_0[n])]
                + [add_low(live.back_1[1 + n], live.kv_1[n])]
            )
        d_projected = jnp.concatenate([part for c in columns for part in c], axis=1)
        live.d_w_qkv = rows_of(d_projected, inputs)
        live.d_projected = d_projected
        del live.back_0, live.back_1, live.kv_0, live.kv_1
        live = fence(live)

        live.vecs = add_low(live.vecs, live.pull.vec_got)
        second_send(live.p3)
        live.p0 = open_plane(live.pull.d_w_qkv, vecs=live.vecs)
        live = fence(live)

        live.vecs = add_low(live.vecs, live.p0.core.pull.whole)
        first_send(live.p0, live.vecs)
        live.closed_3 = close(live.pull.p3)
        live.middle = middle
        live.d_inputs = live.d_hidden + dot_nn(live.d_projected, w_qkv)
        del live.d_projected
        live = fence(live)

        live.vecs = add_low(live.vecs, live.p0.upper.pull.whole)
        second_send(live.p0, live.vecs)
        first, second = live.middle[:share], live.middle[share:]
        live.inner = jnp.where(odd, first, second)
        live.inner_got = swap(jnp.where(odd, second, first), "z", 4, 1)
        del live.middle
        away = far(live.d_inputs[span:].astype(BF16))
        live = fence(live)

        live.vecs = add_low(live.vecs, live.p0.upper.pull.whole)
        lowest = close(live.pull.p0)
        live.outer = jnp.where(odd, live.closed_3, lowest)
        sent = jnp.where(odd, lowest, live.pull.closed_3)
        live.outer_got = swap(jnp.concatenate([sent, live.vecs]), "z", 4, 1)
        live.inner = add_low(live.inner, live.pull.inner_got)
        live.inner_got = lax.ppermute(live.inner, "z", [(3, 1), (0, 2)])
        live = fence(live)

        live.vecs = add_low(live.vecs, live.outer_got[share:])
        live.outer = add_low(live.outer, live.pull.outer_got[:share])
        live.outer_got = lax.ppermute(live.outer, "z", [(2, 0), (1, 3)])
        input_grad = ungroup(live.d_inputs[:span], away.astype(F32))
        owner = ((z_place * ny + y_place) * nx + x_place) * nc + core
        vecs = live.vecs.astype(F32).reshape(-1)
        own_vecs = lax.dynamic_slice(vecs, (owner * share,), (share,))
        live.inner = live.inner.astype(F32) + live.pull.inner_got.astype(F32)
        live = fence(live)

        outer = live.outer.astype(F32) + live.outer_got.astype(F32)
        own_mats = jnp.where((z_place == 0) | (z_place == 3), outer, live.inner)
    else:
        block_out = ungroup(result[:span], far(result[span:]))
        d_hidden, d_branch, d_mixed, d_b_out, d_gain_one, d_shift_one = hidden_back(
            d_inner, d_hidden_two
        )
        d_w_out = rows_of(d_branch, mixed)

        def send_back(mine, others):
            offset = half // 2
            while offset >= 1:
                rows = offset * nc * count
                got = swap(others[rows - count :], "x", nx, offset)
                mine = add_low(mine, got[:count])
                others = add_low(others[: rows - count], got[count:])
                offset //= 2
            return add_low(mine, swap(others, "core", nc, 1))

        columns = [[], [], []]
        for part in range(2):
            d_query, d_key_own, d_value_own, d_key_other, d_value_other = attend_back(
                part, d_mixed
            )
            columns[0].append(d_query)
            columns[1].append(send_back(d_key_own, d_key_other))
            columns[2].append(send_back(d_value_own, d_value_other))
        d_query, _, d_value = (jnp.concatenate(c, axis=1) for c in columns)
        d_projected = jnp.concatenate([part for c in columns for part in c], axis=1)
        d_w_qkv = rows_of(d_projected, inputs)
        d_inputs = d_hidden + dot_nn(d_projected, w_qkv)
        d_away = far(d_inputs[span:].astype(BF16)).astype(F32)
        input_grad = ungroup(d_inputs[:span], d_away)
        grad_rows = jnp.concatenate([d_w_qkv, d_w_out, d_w_first, d_second_low, d_second_high])
        own_mats = lax.psum_scatter(grad_rows, every, scatter_dimension=0, tiled=True)
        own_mats = own_mats.astype(F32)
        grad_vecs = jnp.concatenate(
            [
                jnp.sum(d_query.astype(F32), axis=0),
                jnp.sum(d_value.astype(F32), axis=0),
                d_b_out,
                d_gain_one,
                d_shift_one,
                d_gain_two,
                d_shift_two,
                d_b_second,
                d_b_first,
            ]
        )
        own_vecs = lax.psum_scatter(grad_vecs, every, scatter_dimension=0, tiled=True)

    new_mats, first_mats, later_mats = adamw(
        mats, own_mats.T, moment_mats, second_mats, rate_mats, weight_decay
    )
    new_vecs, first_vecs, later_vecs = adamw(
        vectors, own_vecs, moment_vecs, second_vecs, rate_vecs, 0.0
    )
    return (
        block_out,
        input_grad,
        new_mats,
        first_mats,
        later_mats,
        new_vecs,
        first_vecs,
        later_vecs,
    )


def solution(mesh):
    dp, seq = mesh.shape["dp"], mesh.shape["seq"]
    ny = 2 ** ((dp.bit_length() - 1) // 2)
    sizes = (dp // ny, ny, seq // 2, 2)
    fine = Mesh(mesh.devices.reshape(sizes), ("z", "y", "x", "core"))
    rows, every = ("z", "y"), ("z", "y", "x", "core")
    tokens = P(rows, ("x", "core"), None)
    return jax.shard_map(
        functools.partial(local, sizes),
        mesh=fine,
        in_specs=(
            tokens,
            P(rows, None),
            tokens,
            P(None, every),
            P(every),
            P(None, every),
            P(None, every),
            P(every),
            P(every),
        ),
        out_specs=(
            tokens,
            tokens,
            P(None, every),
            P(None, every),
            P(None, every),
            P(every),
            P(every),
            P(every),
        ),
        check_vma=False,
    )
```

```python
import functools

import jax
import jax.numpy as jnp
from jax import lax
from jax.experimental import pallas as pl
from jax.experimental.pallas import tpu as pltpu
from jax.sharding import Mesh
from jax.sharding import PartitionSpec as P

D = 768
HEADS = 12
HEAD = D // HEADS
FF = 3072
STEP = 10
LANES = 128
PAIRS = D // LANES
FIRST = ((0, 0), (1, 1), (2, 3))
SECOND = ((0, 1), (1, 2))


norm_eps = 1e-05
first_decay = 0.9
second_decay = 0.999
adam_eps = 1e-08
rate_mats = 0.08
rate_vecs = 0.4
weight_decay = 0.01

F32 = jnp.float32
QUICK = pl.CostEstimate(flops=0, bytes_accessed=0, transcendentals=0)
BF16 = jnp.bfloat16


def dot_nn(left, right):
    return lax.dot_general(left, right, (((1,), (0,)), ((), ())), preferred_element_type=F32)


def dot_nt(left, right):
    return lax.dot_general(left, right, (((1,), (1,)), ((), ())), preferred_element_type=F32)


def dot_tn(left, right):
    return lax.dot_general(left, right, (((0,), (0,)), ((), ())), preferred_element_type=F32)


def adamw(weight, gradient, moment, second, rate, decay):
    moment_new = first_decay * moment + (1.0 - first_decay) * gradient
    second_new = second_decay * second + (1.0 - second_decay) * gradient * gradient
    fixed_first = moment_new / (1.0 - first_decay**STEP)
    fixed_second = second_new / (1.0 - second_decay**STEP)
    weight_new = weight - rate * (
        fixed_first / (jnp.sqrt(fixed_second) + adam_eps) + decay * weight
    )
    return (weight_new, moment_new, second_new)


def attend_forward_kernel(
    q_ref, ko_ref, vo_ref, kt_ref, vt_ref, mq_ref, mo_ref, mt_ref, a_ref, e_ref, inv_ref
):
    count = q_ref.shape[0]
    own = ko_ref.shape[0]
    total = own + kt_ref.shape[0]
    q = q_ref[...]
    lane = lax.broadcasted_iota(jnp.int32, (1, LANES), 1)
    row = lax.broadcasted_iota(jnp.int32, (LANES, 1), 0)
    value_t = jnp.concatenate([vo_ref[...].T, vt_ref[...].T], axis=1)
    halves = []
    for h in range(2):
        inside = (lane < HEAD) if h == 0 else (lane >= HEAD)
        inside_row = (row < HEAD) if h == 0 else (row >= HEAD)
        q_h = jnp.where(inside, q, mq_ref[...])
        k_o = jnp.where(inside, ko_ref[...], mo_ref[...])
        k_t = jnp.where(inside, kt_ref[...], mt_ref[...])
        s_o = dot_nt(k_o, q_h)
        s_t = dot_nt(k_t, q_h)
        top = jnp.maximum(
            jnp.max(s_o, axis=0, keepdims=True), jnp.max(s_t, axis=0, keepdims=True)
        )
        e_ref[h, 0:own, :] = jnp.exp(s_o - top).astype(BF16)
        e_ref[h, own:total, :] = jnp.exp(s_t - top).astype(BF16)
        v_h = jnp.where(inside_row, value_t, jnp.ones_like(value_t))
        mixed = dot_nn(v_h, e_ref[h])
        one = HEAD if h == 0 else 0
        inverse = 1.0 / mixed[one : one + 1, :]
        inv_ref[0, h : h + 1, :] = inverse
        halves.append(mixed * inverse)
    both = jnp.where(row < HEAD, halves[0], halves[1])
    a_ref[...] = both.T.astype(BF16)


def attend_forward(q, own, other, mask_q, mask_own, mask_other, first, pairs):
    count = q.shape[0]
    here, there = own.shape[0], other.shape[0]
    place = lambda j: (0, j)
    column = lambda j: (0, j + first)
    shifted = lambda j: (0, j + first + PAIRS)
    whole = lambda j: (0, 0)
    return pl.pallas_call(
        attend_forward_kernel,
        grid=(pairs,),
        in_specs=[
            pl.BlockSpec((count, LANES), column),
            pl.BlockSpec((here, LANES), column),
            pl.BlockSpec((here, LANES), shifted),
            pl.BlockSpec((there, LANES), column),
            pl.BlockSpec((there, LANES), shifted),
            pl.BlockSpec((count, LANES), whole),
            pl.BlockSpec((here, LANES), whole),
            pl.BlockSpec((there, LANES), whole),
        ],
        out_specs=[
            pl.BlockSpec((count, LANES), place),
            pl.BlockSpec((2, here + there, count), lambda j: (j, 0, 0)),
            pl.BlockSpec((1, 2, count), lambda j: (j, 0, 0)),
        ],
        out_shape=[
            jax.ShapeDtypeStruct((count, pairs * LANES), BF16),
            pltpu.HBM((2 * pairs, here + there, count), BF16),
            jax.ShapeDtypeStruct((pairs, 2, count), F32),
        ],
        compiler_params=pltpu.CompilerParams(vmem_limit_bytes=52 * 2**20),
        cost_estimate=QUICK,
        name="attend_forward",
    )(q, own, own, other, other, mask_q, mask_own, mask_other)


def attend_backward_kernel(
    e_ref,
    inv_ref,
    q_ref,
    ko_ref,
    vo_ref,
    kt_ref,
    vt_ref,
    a_ref,
    da_ref,
    dq_ref,
    dko_ref,
    dvo_ref,
    dkt_ref,
    dvt_ref,
    ds_ref,
):
    own = ko_ref.shape[0]
    total = own + kt_ref.shape[0]
    lane = lax.broadcasted_iota(jnp.int32, (1, LANES), 1)
    row = lax.broadcasted_iota(jnp.int32, (LANES, 1), 0)
    da = da_ref[...]
    zero = jnp.zeros_like(da)
    product = (da.astype(F32) * a_ref[...].astype(F32)).T
    inv_t = jnp.where(row < HEAD, inv_ref[0, 0:1, :], inv_ref[0, 1:2, :])
    inverse = inv_t.T
    da_scaled = (da.astype(F32) * inverse).astype(BF16)
    q_scaled = (q_ref[...].astype(F32) * inverse).astype(BF16)
    keys_t = jnp.concatenate([ko_ref[...].T, kt_ref[...].T], axis=1)
    d_value = None
    d_key = None
    halves = []
    for h in range(2):
        inside = (lane < HEAD) if h == 0 else (lane >= HEAD)
        da_h = jnp.where(inside, da, zero)
        delta = jnp.sum(product[h * HEAD : (h + 1) * HEAD, :], axis=0, keepdims=True)
        dp_o = dot_nt(vo_ref[...], da_h)
        ds_ref[h, 0:own, :] = (e_ref[h, 0:own, :].astype(F32) * (dp_o - delta)).astype(BF16)
        dp_t = dot_nt(vt_ref[...], da_h)
        ds_ref[h, own:total, :] = (
            e_ref[h, own:total, :].astype(F32) * (dp_t - delta)
        ).astype(BF16)
        part_v = dot_nn(e_ref[h], jnp.where(inside, da_scaled, zero))
        part_k = dot_nn(ds_ref[h], jnp.where(inside, q_scaled, zero))
        d_value = part_v if d_value is None else d_value + part_v
        d_key = part_k if d_key is None else d_key + part_k
        halves.append(dot_nn(keys_t, ds_ref[h]))
    both = jnp.where(row < HEAD, halves[0], halves[1]) * inv_t
    dq_ref[...] = (both.T * (HEAD**-0.5)).astype(BF16)
    dko_ref[...] = d_key[0:own].astype(BF16)
    dvo_ref[...] = d_value[0:own].astype(BF16)
    dkt_ref[...] = d_key[own:total].astype(BF16)
    dvt_ref[...] = d_value[own:total].astype(BF16)


def attend_backward(e, inverse, q, own, other, a, da, first, pairs):
    count = q.shape[0]
    here, there = own.shape[0], other.shape[0]
    place = lambda j: (0, j)
    column = lambda j: (0, j + first)
    shifted = lambda j: (0, j + first + PAIRS)
    mine = pl.BlockSpec((count, LANES), column)
    width = pairs * LANES
    return pl.pallas_call(
        attend_backward_kernel,
        grid=(pairs,),
        in_specs=[
            pl.BlockSpec((2, here + there, count), lambda j: (j, 0, 0)),
            pl.BlockSpec((1, 2, count), lambda j: (j, 0, 0)),
            mine,
            pl.BlockSpec((here, LANES), column),
            pl.BlockSpec((here, LANES), shifted),
            pl.BlockSpec((there, LANES), column),
            pl.BlockSpec((there, LANES), shifted),
            pl.BlockSpec((count, LANES), place),
            mine,
        ],
        out_specs=[
            pl.BlockSpec((count, LANES), place),
            pl.BlockSpec((here, LANES), place),
            pl.BlockSpec((here, LANES), place),
            pl.BlockSpec((there, LANES), place),
            pl.BlockSpec((there, LANES), place),
        ],
        out_shape=[
            jax.ShapeDtypeStruct((count, width), BF16),
            jax.ShapeDtypeStruct((here, width), BF16),
            jax.ShapeDtypeStruct((here, width), BF16),
            jax.ShapeDtypeStruct((there, width), BF16),
            jax.ShapeDtypeStruct((there, width), BF16),
        ],
        scratch_shapes=[pltpu.VMEM((2, here + there, count), BF16)],
        compiler_params=pltpu.CompilerParams(vmem_limit_bytes=52 * 2**20),
        cost_estimate=QUICK,
        name="attend_backward",
    )(e, inverse, q, own, own, other, other, a, da)


def feed_kernel(y_ref, first_ref, second_ref, b_ref, u_ref, slope_ref, f_ref):
    z = dot_nt(y_ref[...], first_ref[...]) + b_ref[...]
    cdf = 0.5 + 0.5 * lax.erf(z * (0.5**0.5))
    density = jnp.exp(-0.5 * z * z) * 0.3989422804014327
    u = (z * cdf).astype(BF16)
    u_ref[...] = u
    slope_ref[...] = (cdf + z * density).astype(BF16)
    part = dot_nn(u, second_ref[...])

    @pl.when(pl.program_id(0) == 0)
    def _():
        f_ref[...] = part

    @pl.when(pl.program_id(0) > 0)
    def _():
        f_ref[...] += part


def feed_layer(y, rows, b, first, block=D):
    count = y.shape[0]
    whole = pl.BlockSpec((count, D), lambda j: (0, 0))
    column = pl.BlockSpec((count, block), lambda j: (0, j))
    begin = first // block
    return pl.pallas_call(
        feed_kernel,
        grid=(FF // block,),
        in_specs=[
            whole,
            pl.BlockSpec((block, D), lambda j: (j + begin, 0)),
            pl.BlockSpec((block, D), lambda j: (j + begin + FF // block, 0)),
            pl.BlockSpec((1, block), lambda j: (0, j)),
        ],
        out_specs=[column, column, whole],
        out_shape=[
            jax.ShapeDtypeStruct((count, FF), BF16),
            jax.ShapeDtypeStruct((count, FF), BF16),
            jax.ShapeDtypeStruct((count, D), F32),
        ],
        compiler_params=pltpu.CompilerParams(vmem_limit_bytes=30 * 2**20),
        cost_estimate=QUICK,
        name="feed_layer",
    )(y, rows, rows, b)


def project_kernel(x_ref, w_ref, b_ref, q_ref, kv_ref):
    value = (dot_nt(x_ref[...], w_ref[...]) + b_ref[...]).astype(BF16)
    step = pl.program_id(0)

    @pl.when(step == 0)
    def _():
        q_ref[...] = (value.astype(F32) * HEAD**-0.5).astype(BF16)

    @pl.when(step > 0)
    def _():
        kv_ref[...] = value


def project(inputs, rows, bias):
    count = inputs.shape[0]
    return pl.pallas_call(
        project_kernel,
        grid=(3,),
        in_specs=[
            pl.BlockSpec((count, D), lambda j: (0, 0)),
            pl.BlockSpec((D, D), lambda j: (j, 0)),
            pl.BlockSpec((1, D), lambda j: (0, j)),
        ],
        out_specs=[
            pl.BlockSpec((count, D), lambda j: (0, 0)),
            pl.BlockSpec((count, D), lambda j: (0, jnp.maximum(j - 1, 0))),
        ],
        out_shape=[
            jax.ShapeDtypeStruct((count, D), BF16),
            jax.ShapeDtypeStruct((count, 2 * D), BF16),
        ],
        compiler_params=pltpu.CompilerParams(vmem_limit_bytes=32 * 2**20),
        cost_estimate=QUICK,
        name="project",
    )(inputs, rows, bias)


def feed_back_kernel(
    df_ref, y_ref, second_ref, first_ref, u_ref, slope_ref, low_ref, high_ref, dfirst_ref, dy_ref, db_ref
):
    step = pl.program_id(0)
    df = df_ref[...]
    dsecond = dot_tn(u_ref[...], df).astype(BF16)

    @pl.when(step == 0)
    def _():
        low_ref[...] = dsecond

    @pl.when(step > 0)
    def _():
        high_ref[...] = dsecond

    dz = (dot_nt(df, second_ref[...]) * slope_ref[...].astype(F32)).astype(BF16)
    db_ref[...] = jnp.sum(dz.astype(F32), axis=0, keepdims=True)
    dfirst_ref[...] = dot_tn(dz, y_ref[...]).astype(BF16)
    part = dot_nn(dz, first_ref[...])

    @pl.when(step == 0)
    def _():
        dy_ref[...] = part

    @pl.when(step > 0)
    def _():
        dy_ref[...] += part


def feed_back_layer(df, y, rows, first, u, slope):
    count = df.shape[0]
    whole = pl.BlockSpec((count, D), lambda j: (0, 0))
    column = pl.BlockSpec((count, D), lambda j: (0, j))
    begin = first // D
    return pl.pallas_call(
        feed_back_kernel,
        grid=(FF // D,),
        in_specs=[
            whole,
            whole,
            pl.BlockSpec((D, D), lambda j: (j + begin + FF // D, 0)),
            pl.BlockSpec((D, D), lambda j: (j + begin, 0)),
            column,
            column,
        ],
        out_specs=[
            pl.BlockSpec((D, D), lambda j: (0, 0)),
            pl.BlockSpec((D, D), lambda j: (jnp.maximum(j - 1, 0), 0)),
            pl.BlockSpec((D, D), lambda j: (j, 0)),
            whole,
            pl.BlockSpec((1, D), lambda j: (0, j)),
        ],
        out_shape=[
            jax.ShapeDtypeStruct((D, D), BF16),
            jax.ShapeDtypeStruct((FF - D, D), BF16),
            jax.ShapeDtypeStruct((FF, D), BF16),
            jax.ShapeDtypeStruct((count, D), F32),
            jax.ShapeDtypeStruct((1, FF), F32),
        ],
        compiler_params=pltpu.CompilerParams(vmem_limit_bytes=32 * 2**20),
        cost_estimate=QUICK,
        name="feed_back",
    )(df, y, rows, rows, u, slope)


def pack_kernel(width, *refs):
    *sources, out_ref = refs
    sums = [jnp.sum(ref[...].astype(F32), axis=0, keepdims=True) for ref in sources[:6]]
    out_ref[...] = jnp.zeros_like(out_ref)
    out_ref[0:1, :width] = sums[0].astype(BF16)
    out_ref[0:1, width:] = sums[1].astype(BF16)
    out_ref[1:2, :width] = (sums[2] + sums[3]).astype(BF16)
    out_ref[1:2, width:] = (sums[4] + sums[5]).astype(BF16)
    row = 2
    for ref in sources[6:]:
        for part in range(ref.shape[1] // D):
            out_ref[row : row + 1, :] = ref[:, part * D : (part + 1) * D].astype(BF16)
            row += 1


def pack_vectors(backs, others):
    (q_0, _, v_0, _, far_0), (q_1, _, v_1, _, far_1) = backs
    others = [other.reshape(1, -1) for other in others]
    return pl.pallas_call(
        functools.partial(pack_kernel, q_0.shape[1]),
        out_shape=jax.ShapeDtypeStruct((16, D), BF16),
        compiler_params=pltpu.CompilerParams(vmem_limit_bytes=32 * 2**20),
        cost_estimate=QUICK,
        name="pack_vectors",
    )(q_0, q_1, v_0, far_0, v_1, far_1, *others)


def partners(size, offset):
    return [(i, i ^ offset) for i in range(size)]


def swap(value, axis, size, offset):
    return lax.ppermute(value, axis, partners(size, offset))


def add_low(left, right):
    return (left.astype(F32) + right.astype(F32)).astype(BF16)


def assemble(found, share, sizes):
    ny, nx, nc = sizes
    owners = ny * nx * nc

    def target(offset):
        dy, dx, dc = offset
        y = lax.axis_index("y") ^ dy
        x = lax.axis_index("x") ^ dx
        core = lax.axis_index("core") ^ dc
        return (y * nx + x) * nc + core

    arrays = []
    for array, *_ in found:
        if not any(array is other for other in arrays):
            arrays.append(array)
    places = [next(i for i, o in enumerate(arrays) if o is f[0]) for f in found]

    def kernel(*refs):
        sources = refs[: len(arrays)]
        out, out_vec, sems, sems_vec = refs[len(arrays) :]
        copies = []
        for n, (array, k, offset, first) in enumerate(found):
            count = min(array.shape[1], share - first)
            source = sources[places[n]]
            start = pl.multiple_of(target(offset) * share + first, 16)
            copies.append(
                pltpu.make_async_copy(
                    source.at[k, pl.ds(0, count), :], out.at[pl.ds(start, count), :], sems.at[n]
                )
            )
            if count < array.shape[1]:
                start = pl.multiple_of(target(offset) * 16, 16)
                copies.append(
                    pltpu.make_async_copy(
                        source.at[k, pl.ds(count, 16), :],
                        out_vec.at[pl.ds(start, 16), :],
                        sems_vec.at[n],
                    )
                )
        for copy in copies:
            copy.start()
        for copy in copies:
            copy.wait()

    inside = pl.BlockSpec(memory_space=pltpu.VMEM)
    return pl.pallas_call(
        kernel,
        in_specs=[pl.BlockSpec(memory_space=pl.ANY)] * len(arrays),
        out_specs=[inside] * 2,
        out_shape=[
            jax.ShapeDtypeStruct((owners * share, D), BF16),
            jax.ShapeDtypeStruct((owners * 16, D), BF16),
        ],
        scratch_shapes=[
            pltpu.SemaphoreType.DMA((len(found),)),
            pltpu.SemaphoreType.DMA((len(found),)),
        ],
        compiler_params=pltpu.CompilerParams(vmem_limit_bytes=16 * 2**20),
        cost_estimate=QUICK,
        name="assemble",
    )(*arrays)


class Pull:
    def __init__(self, bag):
        self.bag = bag

    def __getattr__(self, name):
        return self.bag.pop(name)


class Bag(dict):
    __setattr__ = dict.__setitem__
    __delattr__ = dict.__delitem__
    pull = property(Pull)

    def __getattr__(self, name):
        return self[name]


def plain(value):
    return {k: plain(v) for k, v in value.items()} if isinstance(value, dict) else value


def bagged(value):
    return Bag({k: bagged(v) for k, v in value.items()}) if isinstance(value, dict) else value


def fence(live):
    return bagged(lax.optimization_barrier(plain(live)))


def plane_start(block, cut):
    return Bag(parts=[block[None, :cut], block[None, cut:]])


def plane_first(plane):
    upper, lower = plane.parts
    plane.got = [swap(upper, "x", 2, 1), swap(lower, "y", 2, 1)]


def plane_second(plane):
    pairs = [jnp.concatenate(both) for both in zip(plane.pull.parts, plane.pull.got)]
    plane.own = pairs + [swap(pairs[0], "y", 2, 1), swap(pairs[1], "x", 2, 1)]


def plane_cores(plane):
    plane.other = [swap(array, "core", 2, 1) for array in plane.own]


def plane_found(plane, cut):
    places = [((0, 0), (0, 1)), ((0, 0), (1, 0)), ((1, 0), (1, 1)), ((0, 1), (1, 1))]
    found = []
    for core, arrays in enumerate((plane.own, plane.other)):
        for n, (array, offsets) in enumerate(zip(arrays, places)):
            for k, offset in enumerate(offsets):
                found.append((array, k, (*offset, core), 0 if n % 2 == 0 else cut))
    return found


def take(value, index, dim):
    return lax.dynamic_index_in_dim(value, index, dim, keepdims=False)


def half_send(value, dim, axis, whole=None):
    place = lax.axis_index(axis)
    away = take(value, 1 - place, dim)
    if whole is None:
        return Bag(all=value, got=swap(away, axis, 2, 1))
    rows = jnp.concatenate([away.reshape(-1, D), whole])
    return Bag(all=value, got=swap(rows, axis, 2, 1))


def half_add(sent, dim, axis):
    keep = take(sent.all, lax.axis_index(axis), dim)
    got = sent.got
    if got.shape != keep.shape:
        got = got[:-16].reshape(keep.shape)
    return add_low(keep, got)


def norm(values, gain, shift):
    center = values - jnp.mean(values, axis=-1, keepdims=True)
    spread_ = jnp.mean(center * center, axis=-1, keepdims=True)
    rate = lax.rsqrt(spread_ + norm_eps)
    unit = center * rate
    return unit * gain + shift, unit, rate


def norm_back(cotangent, unit, rate, gain):
    scaled = cotangent * gain
    mean = jnp.mean(scaled, axis=-1, keepdims=True)
    along = jnp.mean(scaled * unit, axis=-1, keepdims=True)
    grad = rate * (scaled - mean - unit * along)
    return grad, jnp.sum(cotangent * unit, axis=0), jnp.sum(cotangent, axis=0)


def local(
    sizes,
    tokens,
    lengths,
    out_grad,
    mats,
    vectors,
    moment_mats,
    second_mats,
    moment_vecs,
    second_vecs,
):
    nz, ny, nx, nc = sizes
    flat = (ny, nx, nc)
    sequences, span, _ = tokens.shape
    share = mats.shape[1]
    cut = share // 2 // 16 * 16
    x_place, core = lax.axis_index("x"), lax.axis_index("core")
    half = nx // 2
    side = x_place // half

    def regroup(value):
        mine = lax.dynamic_index_in_dim(value, side, 0, keepdims=False)
        away = lax.dynamic_index_in_dim(value, 1 - side, 0, keepdims=False)
        return mine, away

    def far(value):
        return swap(value, "x", nx, half)

    def ungroup(mine, got):
        low, high = (jnp.stack([mine, got]), jnp.stack([got, mine]))
        return jnp.where(side == 0, low, high)

    count = sequences * span

    ends = jnp.cumsum(lax.dynamic_index_in_dim(lengths, side, 0, keepdims=False))

    def documents(offset_x, offset_core):
        at = lax.broadcasted_iota(jnp.int32, (2, span), 1)
        part = lax.broadcasted_iota(jnp.int32, (2, span), 0)
        x_at = x_place ^ offset_x ^ (part * half)
        at = ((x_at * nc) + (core ^ offset_core)) * span + at
        at = at.reshape(-1, 1)
        return jnp.sum((at >= ends[None, :]).astype(jnp.int32), axis=-1, keepdims=True)

    slot = lax.broadcasted_iota(jnp.int32, (1, LANES), 1) % HEAD
    group = [(dx, dc) for dx in range(half) for dc in range(nc)]
    seg = [documents(dx, dc) for dx, dc in group]
    mask_q = jnp.where(slot == seg[0], -1e30, 0.0).astype(BF16)
    mask_own = (slot != seg[0]).astype(BF16)
    mask_other = (slot != jnp.concatenate(seg[1:])).astype(BF16)
    width = PAIRS // 2

    def attend(part, query, own, other):
        return attend_forward(
            query, own, other, mask_q, mask_own, mask_other, part * width, width
        )

    every = ("z", "y", "x", "core")
    shard = mats.T.astype(BF16)
    token_mine, token_away = regroup(tokens)
    grad_mine, grad_away = regroup(out_grad)

    def project_all(inputs, rows, vec):
        bias = jnp.concatenate([vec[:D], jnp.zeros((D,), F32), vec[D : 2 * D]])
        return project(inputs, rows, bias.reshape(1, -1))

    z_place, y_place = lax.axis_index("z"), lax.axis_index("y")
    if sizes == (4, 2, 2, 2):
        odd = z_place % 2 == 1
        vec = jnp.pad(vectors, (0, D - share)).reshape(1, D).astype(BF16)
        at = lax.broadcasted_iota(jnp.int32, (16, D), 0)
        vec = jnp.where(at == z_place, vec, jnp.zeros_like(vec))

        live = Bag(shard=shard, vec=vec)
        live.got = lax.ppermute(shard, "z", [(0, 2)])
        live.vec_got = swap(vec, "z", 4, 2)
        third, trio = share // 4, [3 * k for k in range(8)]
        large, middle = 3 * third, 2 * third
        rank = ((z_place * ny + y_place) * nx + x_place) * nc + core
        kind = (rank + 1) % 3
        main = jnp.where(kind == 2, shard[third:], shard[:large])
        extra = jnp.where(kind == 0, jnp.concatenate([shard[large:], shard[:third]]), shard[middle:])
        give = [
            lax.ppermute(
                main,
                every,
                [(8 + s + i, r + j) for s, r in zip(trio, range(0, 32, 4)) for i, j in FIRST],
            ),
            lax.ppermute(
                extra,
                every,
                [(8 + s + i, r + j) for s, r in zip(trio, range(0, 32, 4)) for i, j in SECOND],
            ),
            lax.ppermute(
                shard[:third],
                every,
                [(8 + s + 2, r + 2) for s, r in zip(trio, range(0, 32, 4))],
            ),
        ]
        main, extra, last = give
        kind = rank % 4
        held = jnp.where(kind == 1, jnp.concatenate([extra[:third], main[:middle]]), main)
        held = jnp.where(kind == 2, jnp.concatenate([extra, last]), held)
        high = lax.all_gather(held, every, axis=0, tiled=True)
        live.held = held
        live = fence(live)
        del live.held

        live.shard = jnp.where(z_place == 2, live.got, live.shard)
        live.vec = live.vec + live.vec_got
        live.got = lax.ppermute(live.shard, "z", [(0, 1), (2, 3)])
        live.token_far = far(token_away)
        live.vec_got = swap(live.vec, "z", 4, 1)
        live = fence(live)

        block = jnp.where(odd, live.pull.got, live.pull.shard)
        live.plane = plane_start(
            jnp.concatenate([block, live.pull.vec + live.pull.vec_got]), cut
        )
        plane_first(live.plane)
        plane_second(live.plane)
        live = fence(live)

        plane_cores(live.plane)
        live.inputs = jnp.concatenate([token_mine, live.pull.token_far])
        live = fence(live)

        low, vecs = assemble(plane_found(live.pull.plane, cut), share, flat)
        vecs = vecs.reshape(-1, 16, D)[:, :nz, :share]
        live.biases = vecs.transpose(1, 0, 2).reshape(-1).astype(F32)
        live.query, live.key_value = project_all(live.inputs, low, live.biases)
        live = fence(live)

        live.kv_got = swap(live.key_value, "core", nc, 1)
        live = fence(live)

        grad_far = far(grad_away)
        inputs, query, biases = live.inputs, live.query, live.biases
        own, other = live.key_value, live.kv_got
    else:
        token_far, grad_far = far(token_away), far(grad_away)
        rows = lax.all_gather(shard, every, axis=0, tiled=True)
        low, high = rows[: 3 * D], rows[3 * D :]
        biases = lax.all_gather(vectors.astype(BF16), every, axis=0, tiled=True).astype(F32)
        inputs = jnp.concatenate([token_mine, token_far])
        query, key_value = project_all(inputs, low, biases)
        pieces = [key_value, swap(key_value, "core", nc, 1)]
        offset = 1
        while offset < half:
            sent = jnp.concatenate(pieces)
            got = swap(sent, "x", nx, offset)
            pieces = [pieces[0], jnp.concatenate([sent[count:], got])]
            offset *= 2
        own, other = pieces
    forward = [attend(part, query, own, other) for part in range(2)]
    mixed = jnp.concatenate([forward[0][0], forward[1][0]], axis=1)
    mixed, high, grad_far = lax.optimization_barrier((mixed, high, grad_far))
    cotangent_near, cotangent_far = grad_mine, grad_far
    w_qkv, w_out = low, high[:D]
    b_out = biases[2 * D : 3 * D]
    gain_one = biases[3 * D : 4 * D]
    shift_one = biases[4 * D : 5 * D]
    gain_two = biases[5 * D : 6 * D]
    shift_two = biases[6 * D : 7 * D]
    b_second = biases[7 * D : 8 * D]
    b_first = biases[8 * D :]

    inputs_wide = inputs.astype(F32)
    hidden = inputs_wide + dot_nt(mixed, w_out) + b_out
    normed, unit_one, rate_one = norm(hidden, gain_one, shift_one)
    normed_low = normed.astype(BF16)
    active, slope, feed = feed_layer(normed_low, high, b_first.reshape(1, -1), D)
    hidden_two = normed + feed + b_second
    result, unit_two, rate_two = norm(hidden_two, gain_two, shift_two)
    result = result.astype(BF16)

    def total(rows):
        return jnp.sum(rows.astype(F32), axis=0)

    def rows_of(left, right):
        return dot_tn(left, right).astype(BF16)

    def attend_back(part, d_mixed):
        return attend_backward(
            forward[part][1],
            forward[part][2],
            query,
            own,
            other,
            forward[part][0],
            d_mixed,
            part * width,
            width,
        )

    def hidden_back(d_inner, d_hidden_two):
        d_normed = d_hidden_two + d_inner
        d_hidden, d_gain, d_shift = norm_back(d_normed, unit_one, rate_one, gain_one)
        d_branch = d_hidden.astype(BF16)
        d_bias = jnp.sum(d_branch.astype(F32), axis=0)
        return d_hidden, d_branch, dot_nn(d_branch, w_out).astype(BF16), d_bias, d_gain, d_shift

    cotangent = jnp.concatenate([cotangent_near, cotangent_far]).astype(F32)
    d_hidden_two, d_gain_two, d_shift_two = norm_back(cotangent, unit_two, rate_two, gain_two)
    d_feed = d_hidden_two.astype(BF16)
    d_b_second = jnp.sum(d_feed.astype(F32), axis=0)
    d_second_low, d_second_high, d_w_first, d_inner, d_b_first = feed_back_layer(
        d_feed, normed_low, high, D, active, slope
    )
    d_b_first = d_b_first.reshape(-1)

    if sizes == (4, 2, 2, 2):
        def open_plane(block, vecs=None):
            return Bag(core=half_send(block.reshape(ny * nx, nc, share, D), 1, "core", vecs))

        def first_send(plane, vecs=None):
            block = half_add(plane.pull.core, 1, "core").reshape(ny, nx, share, D)
            plane.upper = half_send(block[:, :, :cut], 0, "y", vecs)
            plane.lower = half_send(block[:, :, cut:], 1, "x")

        def second_send(plane, vecs=None):
            plane.upper = half_send(half_add(plane.upper, 0, "y"), 0, "x", vecs)
            plane.lower = half_send(half_add(plane.lower, 1, "x"), 0, "y")

        def close(plane):
            return jnp.concatenate(
                [half_add(plane.upper, 0, "x"), half_add(plane.lower, 0, "y")]
            )

        live = Bag(third=d_second_high, d_w_first=d_w_first, low=d_second_low, result=result)
        live.update(d_inner=d_inner, d_hidden_two=d_hidden_two)
        live = fence(live)

        d_hidden, d_branch, d_mixed, d_b_out, d_gain_one, d_shift_one = hidden_back(
            live.pull.d_inner, live.pull.d_hidden_two
        )
        live.update(d_hidden=d_hidden, d_mixed=d_mixed)
        middle = [rows_of(d_branch, mixed), live.pull.d_w_first, live.pull.low]
        middle = jnp.concatenate(middle).reshape(2, ny * nx * nc, share, D)
        live.middle = middle.transpose(1, 0, 2, 3).reshape(-1, D)
        live = fence(live)

        middle = lax.psum_scatter(
            live.pull.middle, ("y", "x", "core"), scatter_dimension=0, tiled=True
        )
        live.p3 = open_plane(live.pull.third)
        live.far = far(live.result[span:])
        live.back_0 = attend_back(0, live.d_mixed)
        live = fence(live)

        block_out = ungroup(live.pull.result[:span], live.pull.far)
        first_send(live.p3)
        live.kv_0 = [swap(other_, "core", nc, 1) for other_ in live.back_0[3:]]
        live.back_1 = attend_back(1, live.d_mixed)
        live = fence(live)

        live.kv_1 = [swap(other_, "core", nc, 1) for other_ in live.back_1[3:]]
        others = [d_b_out, d_gain_one, d_shift_one, d_gain_two, d_shift_two, d_b_second, d_b_first]
        live.vecs = pack_vectors((live.back_0, live.back_1), others)
        live.vec_got = swap(live.vecs, "z", 4, 2)
        columns = [[back[0] for back in (live.back_0, live.back_1)]]
        for n in range(2):
            columns.append(
                [add_low(live.back_0[1 + n], live.kv_0[n])]
                + [add_low(live.back_1[1 + n], live.kv_1[n])]
            )
        d_projected = jnp.concatenate([part for c in columns for part in c], axis=1)
        live.d_w_qkv = rows_of(d_projected, inputs)
        live.d_projected = d_projected
        del live.back_0, live.back_1, live.kv_0, live.kv_1
        live = fence(live)

        live.vecs = add_low(live.vecs, live.pull.vec_got)
        second_send(live.p3)
        live.p0 = open_plane(live.pull.d_w_qkv, vecs=live.vecs)
        live = fence(live)

        live.vecs = add_low(live.vecs, live.p0.core.got[-16:])
        first_send(live.p0, live.vecs)
        live.closed_3 = close(live.pull.p3)
        live.middle = middle
        live.d_inputs = live.d_hidden + dot_nn(live.d_projected, w_qkv)
        del live.d_projected
        live = fence(live)

        live.vecs = add_low(live.vecs, live.p0.upper.got[-16:])
        second_send(live.p0, live.vecs)
        first, second = live.middle[:share], live.middle[share:]
        live.inner = jnp.where(odd, first, second)
        live.inner_got = swap(jnp.where(odd, second, first), "z", 4, 1)
        del live.middle
        away = far(live.d_inputs[span:].astype(BF16))
        live = fence(live)

        live.vecs = add_low(live.vecs, live.p0.upper.got[-16:])
        lowest = close(live.pull.p0)
        live.outer = jnp.where(odd, live.closed_3, lowest)
        sent = jnp.where(odd, lowest, live.pull.closed_3)
        live.outer_got = swap(jnp.concatenate([sent, live.vecs]), "z", 4, 1)
        live.inner = add_low(live.inner, live.pull.inner_got)
        live.inner_got = lax.ppermute(live.inner, "z", [(3, 1), (0, 2)])
        live = fence(live)

        live.vecs = add_low(live.vecs, live.outer_got[share:])
        live.outer = add_low(live.outer, live.pull.outer_got[:share])
        live.outer_got = lax.ppermute(live.outer, "z", [(2, 0), (1, 3)])
        input_grad = ungroup(live.d_inputs[:span], away.astype(F32))
        owner = ((z_place * ny + y_place) * nx + x_place) * nc + core
        vecs = live.vecs.astype(F32).reshape(-1)
        own_vecs = lax.dynamic_slice(vecs, (owner * share,), (share,))
        live.inner = live.inner.astype(F32) + live.pull.inner_got.astype(F32)
        live = fence(live)

        outer = live.outer.astype(F32) + live.outer_got.astype(F32)
        own_mats = jnp.where((z_place == 0) | (z_place == 3), outer, live.inner)
    else:
        block_out = ungroup(result[:span], far(result[span:]))
        d_hidden, d_branch, d_mixed, d_b_out, d_gain_one, d_shift_one = hidden_back(
            d_inner, d_hidden_two
        )
        d_w_out = rows_of(d_branch, mixed)

        def send_back(mine, others):
            offset = half // 2
            while offset >= 1:
                rows = offset * nc * count
                got = swap(others[rows - count :], "x", nx, offset)
                mine = add_low(mine, got[:count])
                others = add_low(others[: rows - count], got[count:])
                offset //= 2
            return add_low(mine, swap(others, "core", nc, 1))

        columns = [[], [], []]
        for part in range(2):
            d_query, d_key_own, d_value_own, d_key_other, d_value_other = attend_back(
                part, d_mixed
            )
            columns[0].append(d_query)
            columns[1].append(send_back(d_key_own, d_key_other))
            columns[2].append(send_back(d_value_own, d_value_other))
        d_query, _, d_value = (jnp.concatenate(c, axis=1) for c in columns)
        d_projected = jnp.concatenate([part for c in columns for part in c], axis=1)
        d_w_qkv = rows_of(d_projected, inputs)
        d_inputs = d_hidden + dot_nn(d_projected, w_qkv)
        d_away = far(d_inputs[span:].astype(BF16)).astype(F32)
        input_grad = ungroup(d_inputs[:span], d_away)
        grad_rows = jnp.concatenate([d_w_qkv, d_w_out, d_w_first, d_second_low, d_second_high])
        own_mats = lax.psum_scatter(grad_rows, every, scatter_dimension=0, tiled=True)
        own_mats = own_mats.astype(F32)
        grad_vecs = jnp.concatenate(
            [
                jnp.sum(d_query.astype(F32), axis=0),
                jnp.sum(d_value.astype(F32), axis=0),
                d_b_out,
                d_gain_one,
                d_shift_one,
                d_gain_two,
                d_shift_two,
                d_b_second,
                d_b_first,
            ]
        )
        own_vecs = lax.psum_scatter(grad_vecs, every, scatter_dimension=0, tiled=True)

    new_mats, first_mats, later_mats = adamw(
        mats, own_mats.T, moment_mats, second_mats, rate_mats, weight_decay
    )
    new_vecs, first_vecs, later_vecs = adamw(
        vectors, own_vecs, moment_vecs, second_vecs, rate_vecs, 0.0
    )
    return (
        block_out,
        input_grad,
        new_mats,
        first_mats,
        later_mats,
        new_vecs,
        first_vecs,
        later_vecs,
    )


def solution(mesh):
    dp, seq = mesh.shape["dp"], mesh.shape["seq"]
    ny = 2 ** ((dp.bit_length() - 1) // 2)
    sizes = (dp // ny, ny, seq // 2, 2)
    fine = Mesh(mesh.devices.reshape(sizes), ("z", "y", "x", "core"))
    rows, every = ("z", "y"), ("z", "y", "x", "core")
    tokens = P(rows, ("x", "core"), None)
    return jax.shard_map(
        functools.partial(local, sizes),
        mesh=fine,
        in_specs=(
            tokens,
            P(rows, None),
            tokens,
            P(None, every),
            P(every),
            P(None, every),
            P(None, every),
            P(every),
            P(every),
        ),
        out_specs=(
            tokens,
            tokens,
            P(None, every),
            P(None, every),
            P(None, every),
            P(every),
            P(every),
            P(every),
        ),
        check_vma=False,
    )
```

```python
import functools

import jax
import jax.numpy as jnp
from jax import lax
from jax.experimental import pallas as pl
from jax.experimental.pallas import tpu as pltpu
from jax.sharding import Mesh
from jax.sharding import PartitionSpec as P

D = 768
HEADS = 12
HEAD = D // HEADS
FF = 3072
STEP = 10
LANES = 128
PAIRS = D // LANES
FIRST = ((0, 0), (1, 1), (2, 3))
SECOND = ((0, 1), (1, 2))


norm_eps = 1e-05
first_decay = 0.9
second_decay = 0.999
adam_eps = 1e-08
rate_mats = 0.08
rate_vecs = 0.4
weight_decay = 0.01

F32 = jnp.float32
QUICK = pl.CostEstimate(flops=0, bytes_accessed=0, transcendentals=0)
BF16 = jnp.bfloat16


def dot_nn(left, right):
    return lax.dot_general(left, right, (((1,), (0,)), ((), ())), preferred_element_type=F32)


def dot_nt(left, right):
    return lax.dot_general(left, right, (((1,), (1,)), ((), ())), preferred_element_type=F32)


def dot_tn(left, right):
    return lax.dot_general(left, right, (((0,), (0,)), ((), ())), preferred_element_type=F32)


def adamw(weight, gradient, moment, second, rate, decay):
    moment_new = first_decay * moment + (1.0 - first_decay) * gradient
    second_new = second_decay * second + (1.0 - second_decay) * gradient * gradient
    fixed_first = moment_new / (1.0 - first_decay**STEP)
    fixed_second = second_new / (1.0 - second_decay**STEP)
    weight_new = weight - rate * (
        fixed_first / (jnp.sqrt(fixed_second) + adam_eps) + decay * weight
    )
    return (weight_new, moment_new, second_new)


def attend_forward_kernel(
    q_ref, ko_ref, vo_ref, kt_ref, vt_ref, mq_ref, mo_ref, mt_ref, a_ref, e_ref, inv_ref
):
    count = q_ref.shape[0]
    own = ko_ref.shape[0]
    total = own + kt_ref.shape[0]
    q = q_ref[...]
    lane = lax.broadcasted_iota(jnp.int32, (1, LANES), 1)
    row = lax.broadcasted_iota(jnp.int32, (LANES, 1), 0)
    value_t = jnp.concatenate([vo_ref[...].T, vt_ref[...].T], axis=1)
    halves = []
    for h in range(2):
        inside = (lane < HEAD) if h == 0 else (lane >= HEAD)
        inside_row = (row < HEAD) if h == 0 else (row >= HEAD)
        q_h = jnp.where(inside, q, mq_ref[...])
        k_o = jnp.where(inside, ko_ref[...], mo_ref[...])
        k_t = jnp.where(inside, kt_ref[...], mt_ref[...])
        s_o = dot_nt(k_o, q_h)
        s_t = dot_nt(k_t, q_h)
        top = jnp.maximum(
            jnp.max(s_o, axis=0, keepdims=True), jnp.max(s_t, axis=0, keepdims=True)
        )
        e_ref[h, 0:own, :] = jnp.exp(s_o - top).astype(BF16)
        e_ref[h, own:total, :] = jnp.exp(s_t - top).astype(BF16)
        v_h = jnp.where(inside_row, value_t, jnp.ones_like(value_t))
        mixed = dot_nn(v_h, e_ref[h])
        one = HEAD if h == 0 else 0
        inverse = 1.0 / mixed[one : one + 1, :]
        inv_ref[0, h : h + 1, :] = inverse
        halves.append(mixed * inverse)
    both = jnp.where(row < HEAD, halves[0], halves[1])
    a_ref[...] = both.T.astype(BF16)


def attend_forward(q, own, other, mask_q, mask_own, mask_other, first, pairs):
    count = q.shape[0]
    here, there = own.shape[0], other.shape[0]
    place = lambda j: (0, j)
    column = lambda j: (0, j + first)
    shifted = lambda j: (0, j + first + PAIRS)
    whole = lambda j: (0, 0)
    return pl.pallas_call(
        attend_forward_kernel,
        grid=(pairs,),
        in_specs=[
            pl.BlockSpec((count, LANES), column),
            pl.BlockSpec((here, LANES), column),
            pl.BlockSpec((here, LANES), shifted),
            pl.BlockSpec((there, LANES), column),
            pl.BlockSpec((there, LANES), shifted),
            pl.BlockSpec((count, LANES), whole),
            pl.BlockSpec((here, LANES), whole),
            pl.BlockSpec((there, LANES), whole),
        ],
        out_specs=[
            pl.BlockSpec((count, LANES), place),
            pl.BlockSpec((2, here + there, count), lambda j: (j, 0, 0)),
            pl.BlockSpec((1, 2, count), lambda j: (j, 0, 0)),
        ],
        out_shape=[
            jax.ShapeDtypeStruct((count, pairs * LANES), BF16),
            pltpu.HBM((2 * pairs, here + there, count), BF16),
            jax.ShapeDtypeStruct((pairs, 2, count), F32),
        ],
        compiler_params=pltpu.CompilerParams(vmem_limit_bytes=52 * 2**20),
        cost_estimate=QUICK,
        name="attend_forward",
    )(q, own, own, other, other, mask_q, mask_own, mask_other)


def attend_backward_kernel(
    e_ref,
    inv_ref,
    q_ref,
    ko_ref,
    vo_ref,
    kt_ref,
    vt_ref,
    a_ref,
    da_ref,
    dq_ref,
    dko_ref,
    dvo_ref,
    dkt_ref,
    dvt_ref,
    ds_ref,
):
    own = ko_ref.shape[0]
    total = own + kt_ref.shape[0]
    lane = lax.broadcasted_iota(jnp.int32, (1, LANES), 1)
    row = lax.broadcasted_iota(jnp.int32, (LANES, 1), 0)
    da = da_ref[...]
    zero = jnp.zeros_like(da)
    product = (da.astype(F32) * a_ref[...].astype(F32)).T
    inv_t = jnp.where(row < HEAD, inv_ref[0, 0:1, :], inv_ref[0, 1:2, :])
    inverse = inv_t.T
    da_scaled = (da.astype(F32) * inverse).astype(BF16)
    q_scaled = (q_ref[...].astype(F32) * inverse).astype(BF16)
    keys_t = jnp.concatenate([ko_ref[...].T, kt_ref[...].T], axis=1)
    d_value = None
    d_key = None
    halves = []
    for h in range(2):
        inside = (lane < HEAD) if h == 0 else (lane >= HEAD)
        da_h = jnp.where(inside, da, zero)
        delta = jnp.sum(product[h * HEAD : (h + 1) * HEAD, :], axis=0, keepdims=True)
        dp_o = dot_nt(vo_ref[...], da_h)
        ds_ref[h, 0:own, :] = (e_ref[h, 0:own, :].astype(F32) * (dp_o - delta)).astype(BF16)
        dp_t = dot_nt(vt_ref[...], da_h)
        ds_ref[h, own:total, :] = (
            e_ref[h, own:total, :].astype(F32) * (dp_t - delta)
        ).astype(BF16)
        part_v = dot_nn(e_ref[h], jnp.where(inside, da_scaled, zero))
        part_k = dot_nn(ds_ref[h], jnp.where(inside, q_scaled, zero))
        d_value = part_v if d_value is None else d_value + part_v
        d_key = part_k if d_key is None else d_key + part_k
        halves.append(dot_nn(keys_t, ds_ref[h]))
    both = jnp.where(row < HEAD, halves[0], halves[1]) * inv_t
    dq_ref[...] = (both.T * (HEAD**-0.5)).astype(BF16)
    dko_ref[...] = d_key[0:own].astype(BF16)
    dvo_ref[...] = d_value[0:own].astype(BF16)
    dkt_ref[...] = d_key[own:total].astype(BF16)
    dvt_ref[...] = d_value[own:total].astype(BF16)


def attend_backward(e, inverse, q, own, other, a, da, first, pairs):
    count = q.shape[0]
    here, there = own.shape[0], other.shape[0]
    place = lambda j: (0, j)
    column = lambda j: (0, j + first)
    shifted = lambda j: (0, j + first + PAIRS)
    mine = pl.BlockSpec((count, LANES), column)
    width = pairs * LANES
    return pl.pallas_call(
        attend_backward_kernel,
        grid=(pairs,),
        in_specs=[
            pl.BlockSpec((2, here + there, count), lambda j: (j, 0, 0)),
            pl.BlockSpec((1, 2, count), lambda j: (j, 0, 0)),
            mine,
            pl.BlockSpec((here, LANES), column),
            pl.BlockSpec((here, LANES), shifted),
            pl.BlockSpec((there, LANES), column),
            pl.BlockSpec((there, LANES), shifted),
            pl.BlockSpec((count, LANES), place),
            mine,
        ],
        out_specs=[
            pl.BlockSpec((count, LANES), place),
            pl.BlockSpec((here, LANES), place),
            pl.BlockSpec((here, LANES), place),
            pl.BlockSpec((there, LANES), place),
            pl.BlockSpec((there, LANES), place),
        ],
        out_shape=[
            jax.ShapeDtypeStruct((count, width), BF16),
            jax.ShapeDtypeStruct((here, width), BF16),
            jax.ShapeDtypeStruct((here, width), BF16),
            jax.ShapeDtypeStruct((there, width), BF16),
            jax.ShapeDtypeStruct((there, width), BF16),
        ],
        scratch_shapes=[pltpu.VMEM((2, here + there, count), BF16)],
        compiler_params=pltpu.CompilerParams(vmem_limit_bytes=52 * 2**20),
        cost_estimate=QUICK,
        name="attend_backward",
    )(e, inverse, q, own, own, other, other, a, da)


def feed_kernel(y_ref, first_ref, second_ref, b_ref, u_ref, slope_ref, f_ref):
    z = dot_nt(y_ref[...], first_ref[...]) + b_ref[...]
    cdf = 0.5 + 0.5 * lax.erf(z * (0.5**0.5))
    density = jnp.exp(-0.5 * z * z) * 0.3989422804014327
    u = (z * cdf).astype(BF16)
    u_ref[...] = u
    slope_ref[...] = (cdf + z * density).astype(BF16)
    part = dot_nn(u, second_ref[...])

    @pl.when(pl.program_id(0) == 0)
    def _():
        f_ref[...] = part

    @pl.when(pl.program_id(0) > 0)
    def _():
        f_ref[...] += part


def feed_layer(y, rows, b, first, block=D):
    count = y.shape[0]
    whole = pl.BlockSpec((count, D), lambda j: (0, 0))
    column = pl.BlockSpec((count, block), lambda j: (0, j))
    begin = first // block
    return pl.pallas_call(
        feed_kernel,
        grid=(FF // block,),
        in_specs=[
            whole,
            pl.BlockSpec((block, D), lambda j: (j + begin, 0)),
            pl.BlockSpec((block, D), lambda j: (j + begin + FF // block, 0)),
            pl.BlockSpec((1, block), lambda j: (0, j)),
        ],
        out_specs=[column, column, whole],
        out_shape=[
            jax.ShapeDtypeStruct((count, FF), BF16),
            jax.ShapeDtypeStruct((count, FF), BF16),
            jax.ShapeDtypeStruct((count, D), F32),
        ],
        compiler_params=pltpu.CompilerParams(vmem_limit_bytes=30 * 2**20),
        cost_estimate=QUICK,
        name="feed_layer",
    )(y, rows, rows, b)


def project_kernel(x_ref, w_ref, b_ref, q_ref, kv_ref):
    value = (dot_nt(x_ref[...], w_ref[...]) + b_ref[...]).astype(BF16)
    step = pl.program_id(0)

    @pl.when(step == 0)
    def _():
        q_ref[...] = (value.astype(F32) * HEAD**-0.5).astype(BF16)

    @pl.when(step > 0)
    def _():
        kv_ref[...] = value


def project(inputs, rows, bias):
    count = inputs.shape[0]
    return pl.pallas_call(
        project_kernel,
        grid=(3,),
        in_specs=[
            pl.BlockSpec((count, D), lambda j: (0, 0)),
            pl.BlockSpec((D, D), lambda j: (j, 0)),
            pl.BlockSpec((1, D), lambda j: (0, j)),
        ],
        out_specs=[
            pl.BlockSpec((count, D), lambda j: (0, 0)),
            pl.BlockSpec((count, D), lambda j: (0, jnp.maximum(j - 1, 0))),
        ],
        out_shape=[
            jax.ShapeDtypeStruct((count, D), BF16),
            jax.ShapeDtypeStruct((count, 2 * D), BF16),
        ],
        compiler_params=pltpu.CompilerParams(vmem_limit_bytes=32 * 2**20),
        cost_estimate=QUICK,
        name="project",
    )(inputs, rows, bias)


def feed_back_kernel(
    df_ref, y_ref, second_ref, first_ref, u_ref, slope_ref, low_ref, high_ref, dfirst_ref, dy_ref, db_ref
):
    step = pl.program_id(0)
    df = df_ref[...]
    dsecond = dot_tn(u_ref[...], df).astype(BF16)

    @pl.when(step == 0)
    def _():
        low_ref[...] = dsecond

    @pl.when(step > 0)
    def _():
        high_ref[...] = dsecond

    dz = (dot_nt(df, second_ref[...]) * slope_ref[...].astype(F32)).astype(BF16)
    db_ref[...] = jnp.sum(dz.astype(F32), axis=0, keepdims=True)
    dfirst_ref[...] = dot_tn(dz, y_ref[...]).astype(BF16)
    part = dot_nn(dz, first_ref[...])

    @pl.when(step == 0)
    def _():
        dy_ref[...] = part

    @pl.when(step > 0)
    def _():
        dy_ref[...] += part


def feed_back_layer(df, y, rows, first, u, slope):
    count = df.shape[0]
    whole = pl.BlockSpec((count, D), lambda j: (0, 0))
    column = pl.BlockSpec((count, D), lambda j: (0, j))
    begin = first // D
    return pl.pallas_call(
        feed_back_kernel,
        grid=(FF // D,),
        in_specs=[
            whole,
            whole,
            pl.BlockSpec((D, D), lambda j: (j + begin + FF // D, 0)),
            pl.BlockSpec((D, D), lambda j: (j + begin, 0)),
            column,
            column,
        ],
        out_specs=[
            pl.BlockSpec((D, D), lambda j: (0, 0)),
            pl.BlockSpec((D, D), lambda j: (jnp.maximum(j - 1, 0), 0)),
            pl.BlockSpec((D, D), lambda j: (j, 0)),
            whole,
            pl.BlockSpec((1, D), lambda j: (0, j)),
        ],
        out_shape=[
            jax.ShapeDtypeStruct((D, D), BF16),
            jax.ShapeDtypeStruct((FF - D, D), BF16),
            jax.ShapeDtypeStruct((FF, D), BF16),
            jax.ShapeDtypeStruct((count, D), F32),
            jax.ShapeDtypeStruct((1, FF), F32),
        ],
        compiler_params=pltpu.CompilerParams(vmem_limit_bytes=32 * 2**20),
        cost_estimate=QUICK,
        name="feed_back",
    )(df, y, rows, rows, u, slope)


def pack_kernel(width, *refs):
    *sources, out_ref = refs
    sums = [jnp.sum(ref[...].astype(F32), axis=0, keepdims=True) for ref in sources[:6]]
    out_ref[...] = jnp.zeros_like(out_ref)
    out_ref[0:1, :width] = sums[0].astype(BF16)
    out_ref[0:1, width:] = sums[1].astype(BF16)
    out_ref[1:2, :width] = (sums[2] + sums[3]).astype(BF16)
    out_ref[1:2, width:] = (sums[4] + sums[5]).astype(BF16)
    row = 2
    for ref in sources[6:]:
        for part in range(ref.shape[1] // D):
            out_ref[row : row + 1, :] = ref[:, part * D : (part + 1) * D].astype(BF16)
            row += 1


def pack_vectors(backs, others):
    (q_0, _, v_0, _, far_0), (q_1, _, v_1, _, far_1) = backs
    others = [other.reshape(1, -1) for other in others]
    return pl.pallas_call(
        functools.partial(pack_kernel, q_0.shape[1]),
        out_shape=jax.ShapeDtypeStruct((16, D), BF16),
        compiler_params=pltpu.CompilerParams(vmem_limit_bytes=32 * 2**20),
        cost_estimate=QUICK,
        name="pack_vectors",
    )(q_0, q_1, v_0, far_0, v_1, far_1, *others)


def partners(size, offset):
    return [(i, i ^ offset) for i in range(size)]


def swap(value, axis, size, offset):
    return lax.ppermute(value, axis, partners(size, offset))


def add_low(left, right):
    return (left.astype(F32) + right.astype(F32)).astype(BF16)


def assemble(found, share, sizes):
    ny, nx, nc = sizes
    owners = ny * nx * nc

    def target(offset):
        dy, dx, dc = offset
        y = lax.axis_index("y") ^ dy
        x = lax.axis_index("x") ^ dx
        core = lax.axis_index("core") ^ dc
        return (y * nx + x) * nc + core

    arrays = []
    for array, *_ in found:
        if not any(array is other for other in arrays):
            arrays.append(array)
    places = [next(i for i, o in enumerate(arrays) if o is f[0]) for f in found]

    def kernel(*refs):
        sources = refs[: len(arrays)]
        out, out_vec, sems, sems_vec = refs[len(arrays) :]
        copies = []
        for n, (array, k, offset, first) in enumerate(found):
            count = min(array.shape[1], share - first)
            source = sources[places[n]]
            start = pl.multiple_of(target(offset) * share + first, 16)
            copies.append(
                pltpu.make_async_copy(
                    source.at[k, pl.ds(0, count), :], out.at[pl.ds(start, count), :], sems.at[n]
                )
            )
            if count < array.shape[1]:
                start = pl.multiple_of(target(offset) * 16, 16)
                copies.append(
                    pltpu.make_async_copy(
                        source.at[k, pl.ds(count, 16), :],
                        out_vec.at[pl.ds(start, 16), :],
                        sems_vec.at[n],
                    )
                )
        for copy in copies:
            copy.start()
        for copy in copies:
            copy.wait()

    inside = pl.BlockSpec(memory_space=pltpu.VMEM)
    return pl.pallas_call(
        kernel,
        in_specs=[pl.BlockSpec(memory_space=pl.ANY)] * len(arrays),
        out_specs=[inside] * 2,
        out_shape=[
            jax.ShapeDtypeStruct((owners * share, D), BF16),
            jax.ShapeDtypeStruct((owners * 16, D), BF16),
        ],
        scratch_shapes=[
            pltpu.SemaphoreType.DMA((len(found),)),
            pltpu.SemaphoreType.DMA((len(found),)),
        ],
        compiler_params=pltpu.CompilerParams(vmem_limit_bytes=16 * 2**20),
        cost_estimate=QUICK,
        name="assemble",
    )(*arrays)


class Pull:
    def __init__(self, bag):
        self.bag = bag

    def __getattr__(self, name):
        return self.bag.pop(name)


class Bag(dict):
    __setattr__ = dict.__setitem__
    __delattr__ = dict.__delitem__
    pull = property(Pull)

    def __getattr__(self, name):
        return self[name]


def plain(value):
    return {k: plain(v) for k, v in value.items()} if isinstance(value, dict) else value


def bagged(value):
    return Bag({k: bagged(v) for k, v in value.items()}) if isinstance(value, dict) else value


def fence(live):
    return bagged(lax.optimization_barrier(plain(live)))


def plane_start(block, cut):
    return Bag(parts=[block[None, :cut], block[None, cut:]])


def plane_first(plane):
    upper, lower = plane.parts
    plane.got = [swap(upper, "x", 2, 1), swap(lower, "y", 2, 1)]


def plane_second(plane):
    pairs = [jnp.concatenate(both) for both in zip(plane.pull.parts, plane.pull.got)]
    plane.own = pairs + [swap(pairs[0], "y", 2, 1), swap(pairs[1], "x", 2, 1)]


def plane_cores(plane):
    plane.other = [swap(array, "core", 2, 1) for array in plane.own]


def plane_found(plane, cut):
    places = [((0, 0), (0, 1)), ((0, 0), (1, 0)), ((1, 0), (1, 1)), ((0, 1), (1, 1))]
    found = []
    for core, arrays in enumerate((plane.own, plane.other)):
        for n, (array, offsets) in enumerate(zip(arrays, places)):
            for k, offset in enumerate(offsets):
                found.append((array, k, (*offset, core), 0 if n % 2 == 0 else cut))
    return found


def take(value, index, dim):
    return lax.dynamic_index_in_dim(value, index, dim, keepdims=False)


def half_send(value, dim, axis, whole=None):
    place = lax.axis_index(axis)
    away = take(value, 1 - place, dim)
    if whole is None:
        return Bag(all=value, got=swap(away, axis, 2, 1))
    rows = jnp.concatenate([away.reshape(-1, D), whole])
    return Bag(all=value, got=swap(rows, axis, 2, 1))


def half_add(sent, dim, axis):
    keep = take(sent.all, lax.axis_index(axis), dim)
    got = sent.got
    if got.shape != keep.shape:
        got = got[:-16].reshape(keep.shape)
    return add_low(keep, got)


def norm(values, gain, shift):
    center = values - jnp.mean(values, axis=-1, keepdims=True)
    spread_ = jnp.mean(center * center, axis=-1, keepdims=True)
    rate = lax.rsqrt(spread_ + norm_eps)
    unit = center * rate
    return unit * gain + shift, unit, rate


def norm_back(cotangent, unit, rate, gain):
    scaled = cotangent * gain
    mean = jnp.mean(scaled, axis=-1, keepdims=True)
    along = jnp.mean(scaled * unit, axis=-1, keepdims=True)
    grad = rate * (scaled - mean - unit * along)
    return grad, jnp.sum(cotangent * unit, axis=0), jnp.sum(cotangent, axis=0)


def local(
    sizes,
    tokens,
    lengths,
    out_grad,
    mats,
    vectors,
    moment_mats,
    second_mats,
    moment_vecs,
    second_vecs,
):
    nz, ny, nx, nc = sizes
    flat = (ny, nx, nc)
    sequences, span, _ = tokens.shape
    share = mats.shape[1]
    cut = share // 2 // 16 * 16
    x_place, core = lax.axis_index("x"), lax.axis_index("core")
    half = nx // 2
    side = x_place // half

    def regroup(value):
        mine = lax.dynamic_index_in_dim(value, side, 0, keepdims=False)
        away = lax.dynamic_index_in_dim(value, 1 - side, 0, keepdims=False)
        return mine, away

    def far(value):
        return swap(value, "x", nx, half)

    def ungroup(mine, got):
        low, high = (jnp.stack([mine, got]), jnp.stack([got, mine]))
        return jnp.where(side == 0, low, high)

    count = sequences * span

    ends = jnp.cumsum(lax.dynamic_index_in_dim(lengths, side, 0, keepdims=False))

    def documents(offset_x, offset_core):
        at = lax.broadcasted_iota(jnp.int32, (2, span), 1)
        part = lax.broadcasted_iota(jnp.int32, (2, span), 0)
        x_at = x_place ^ offset_x ^ (part * half)
        at = ((x_at * nc) + (core ^ offset_core)) * span + at
        at = at.reshape(-1, 1)
        return jnp.sum((at >= ends[None, :]).astype(jnp.int32), axis=-1, keepdims=True)

    slot = lax.broadcasted_iota(jnp.int32, (1, LANES), 1) % HEAD
    group = [(dx, dc) for dx in range(half) for dc in range(nc)]
    seg = [documents(dx, dc) for dx, dc in group]
    mask_q = jnp.where(slot == seg[0], -1e30, 0.0).astype(BF16)
    mask_own = (slot != seg[0]).astype(BF16)
    mask_other = (slot != jnp.concatenate(seg[1:])).astype(BF16)
    width = PAIRS // 2

    def attend(part, query, own, other):
        return attend_forward(
            query, own, other, mask_q, mask_own, mask_other, part * width, width
        )

    every = ("z", "y", "x", "core")
    shard = mats.T.astype(BF16)
    token_mine, token_away = regroup(tokens)
    grad_mine, grad_away = regroup(out_grad)

    def project_all(inputs, rows, vec):
        bias = jnp.concatenate([vec[:D], jnp.zeros((D,), F32), vec[D : 2 * D]])
        return project(inputs, rows, bias.reshape(1, -1))

    z_place, y_place = lax.axis_index("z"), lax.axis_index("y")
    if sizes == (4, 2, 2, 2):
        odd = z_place % 2 == 1
        vec = jnp.pad(vectors, (0, D - share)).reshape(1, D).astype(BF16)
        at = lax.broadcasted_iota(jnp.int32, (16, D), 0)
        vec = jnp.where(at == z_place, vec, jnp.zeros_like(vec))

        live = Bag(shard=shard, vec=vec)
        live.got = lax.ppermute(shard, "z", [(0, 2)])
        live.vec_got = swap(vec, "z", 4, 2)
        third, trio = share // 4, [3 * k for k in range(8)]
        large, middle = 3 * third, 2 * third
        rank = ((z_place * ny + y_place) * nx + x_place) * nc + core
        kind = (rank + 1) % 3
        main = jnp.where(kind == 2, shard[third:], shard[:large])
        extra = jnp.where(kind == 0, jnp.concatenate([shard[large:], shard[:third]]), shard[middle:])
        give = [
            lax.ppermute(
                main,
                every,
                [(8 + s + i, r + j) for s, r in zip(trio, range(0, 32, 4)) for i, j in FIRST],
            ),
            lax.ppermute(
                extra,
                every,
                [(8 + s + i, r + j) for s, r in zip(trio, range(0, 32, 4)) for i, j in SECOND],
            ),
            lax.ppermute(
                shard[:third],
                every,
                [(8 + s + 2, r + 2) for s, r in zip(trio, range(0, 32, 4))],
            ),
        ]
        main, extra, last = give
        kind = rank % 4
        held = jnp.where(kind == 1, jnp.concatenate([extra[:third], main[:middle]]), main)
        held = jnp.where(kind == 2, jnp.concatenate([extra, last]), held)
        high = lax.all_gather(held, every, axis=0, tiled=True)
        live.held = held
        live = fence(live)
        del live.held

        live.shard = jnp.where(z_place == 2, live.got, live.shard)
        live.vec = live.vec + live.vec_got
        live.got = lax.ppermute(live.shard, "z", [(0, 1), (2, 3)])
        live.token_far = far(token_away)
        live.vec_got = swap(live.vec, "z", 4, 1)
        live = fence(live)

        block = jnp.where(odd, live.pull.got, live.pull.shard)
        live.plane = plane_start(
            jnp.concatenate([block, live.pull.vec + live.pull.vec_got]), cut
        )
        plane_first(live.plane)
        plane_second(live.plane)
        live = fence(live)

        plane_cores(live.plane)
        live.inputs = jnp.concatenate([token_mine, live.pull.token_far])
        live = fence(live)

        low, vecs = assemble(plane_found(live.pull.plane, cut), share, flat)
        vecs = vecs.reshape(-1, 16, D)[:, :nz, :share]
        live.biases = vecs.transpose(1, 0, 2).reshape(-1).astype(F32)
        live.query, live.key_value = project_all(live.inputs, low, live.biases)
        live = fence(live)

        live.kv_got = swap(live.key_value, "core", nc, 1)
        live = fence(live)

        grad_far = far(grad_away)
        inputs, query, biases = live.inputs, live.query, live.biases
        own, other = live.key_value, live.kv_got
    else:
        token_far, grad_far = far(token_away), far(grad_away)
        rows = lax.all_gather(shard, every, axis=0, tiled=True)
        low, high = rows[: 3 * D], rows[3 * D :]
        biases = lax.all_gather(vectors.astype(BF16), every, axis=0, tiled=True).astype(F32)
        inputs = jnp.concatenate([token_mine, token_far])
        query, key_value = project_all(inputs, low, biases)
        pieces = [key_value, swap(key_value, "core", nc, 1)]
        offset = 1
        while offset < half:
            sent = jnp.concatenate(pieces)
            got = swap(sent, "x", nx, offset)
            pieces = [pieces[0], jnp.concatenate([sent[count:], got])]
            offset *= 2
        own, other = pieces
    forward = [attend(part, query, own, other) for part in range(2)]
    mixed = jnp.concatenate([forward[0][0], forward[1][0]], axis=1)
    mixed, high, grad_far = lax.optimization_barrier((mixed, high, grad_far))
    cotangent_near, cotangent_far = grad_mine, grad_far
    w_qkv, w_out = low, high[:D]
    b_out = biases[2 * D : 3 * D]
    gain_one = biases[3 * D : 4 * D]
    shift_one = biases[4 * D : 5 * D]
    gain_two = biases[5 * D : 6 * D]
    shift_two = biases[6 * D : 7 * D]
    b_second = biases[7 * D : 8 * D]
    b_first = biases[8 * D :]

    inputs_wide = inputs.astype(F32)
    hidden = inputs_wide + dot_nt(mixed, w_out) + b_out
    normed, unit_one, rate_one = norm(hidden, gain_one, shift_one)
    normed_low = normed.astype(BF16)
    active, slope, feed = feed_layer(normed_low, high, b_first.reshape(1, -1), D)
    hidden_two = normed + feed + b_second
    result, unit_two, rate_two = norm(hidden_two, gain_two, shift_two)
    result = result.astype(BF16)

    def total(rows):
        return jnp.sum(rows.astype(F32), axis=0)

    def rows_of(left, right):
        return dot_tn(left, right).astype(BF16)

    def attend_back(part, d_mixed):
        return attend_backward(
            forward[part][1],
            forward[part][2],
            query,
            own,
            other,
            forward[part][0],
            d_mixed,
            part * width,
            width,
        )

    def hidden_back(d_inner, d_hidden_two):
        d_normed = d_hidden_two + d_inner
        d_hidden, d_gain, d_shift = norm_back(d_normed, unit_one, rate_one, gain_one)
        d_branch = d_hidden.astype(BF16)
        d_bias = jnp.sum(d_branch.astype(F32), axis=0)
        return d_hidden, d_branch, dot_nn(d_branch, w_out).astype(BF16), d_bias, d_gain, d_shift

    cotangent = jnp.concatenate([cotangent_near, cotangent_far]).astype(F32)
    d_hidden_two, d_gain_two, d_shift_two = norm_back(cotangent, unit_two, rate_two, gain_two)
    d_feed = d_hidden_two.astype(BF16)
    d_b_second = jnp.sum(d_feed.astype(F32), axis=0)
    d_second_low, d_second_high, d_w_first, d_inner, d_b_first = feed_back_layer(
        d_feed, normed_low, high, D, active, slope
    )
    d_b_first = d_b_first.reshape(-1)

    if sizes == (4, 2, 2, 2):
        def open_plane(block, vecs=None):
            return Bag(core=half_send(block.reshape(ny * nx, nc, share, D), 1, "core", vecs))

        def first_send(plane, vecs=None):
            block = half_add(plane.pull.core, 1, "core").reshape(ny, nx, share, D)
            plane.upper = half_send(block[:, :, :cut], 0, "y", vecs)
            plane.lower = half_send(block[:, :, cut:], 1, "x")

        def second_send(plane, vecs=None):
            plane.upper = half_send(half_add(plane.upper, 0, "y"), 0, "x", vecs)
            plane.lower = half_send(half_add(plane.lower, 1, "x"), 0, "y")

        def close(plane):
            return jnp.concatenate(
                [half_add(plane.upper, 0, "x"), half_add(plane.lower, 0, "y")]
            )

        live = Bag(third=d_second_high, d_w_first=d_w_first, low=d_second_low, result=result)
        live.update(d_inner=d_inner, d_hidden_two=d_hidden_two)
        live = fence(live)

        d_hidden, d_branch, d_mixed, d_b_out, d_gain_one, d_shift_one = hidden_back(
            live.pull.d_inner, live.pull.d_hidden_two
        )
        live.update(d_hidden=d_hidden, d_mixed=d_mixed)
        middle = [rows_of(d_branch, mixed), live.pull.d_w_first, live.pull.low]
        middle = jnp.concatenate(middle).reshape(2, ny * nx * nc, share, D)
        live.middle = middle.transpose(1, 0, 2, 3).reshape(-1, D)
        live = fence(live)

        middle = lax.psum_scatter(
            live.pull.middle, ("y", "x", "core"), scatter_dimension=0, tiled=True
        )
        live.p3 = open_plane(live.pull.third)
        live.back_0 = attend_back(0, live.d_mixed)
        live = fence(live)

        first_send(live.p3)
        live.kv_0 = [swap(other_, "core", nc, 1) for other_ in live.back_0[3:]]
        live.back_1 = attend_back(1, live.d_mixed)
        live = fence(live)

        live.kv_1 = [swap(other_, "core", nc, 1) for other_ in live.back_1[3:]]
        others = [d_b_out, d_gain_one, d_shift_one, d_gain_two, d_shift_two, d_b_second, d_b_first]
        live.vecs = pack_vectors((live.back_0, live.back_1), others)
        live.vec_got = swap(live.vecs, "z", 4, 2)
        columns = [[back[0] for back in (live.back_0, live.back_1)]]
        for n in range(2):
            columns.append(
                [add_low(live.back_0[1 + n], live.kv_0[n])]
                + [add_low(live.back_1[1 + n], live.kv_1[n])]
            )
        d_projected = jnp.concatenate([part for c in columns for part in c], axis=1)
        live.d_w_qkv = rows_of(d_projected, inputs)
        live.d_projected = d_projected
        del live.back_0, live.back_1, live.kv_0, live.kv_1
        live = fence(live)

        live.vecs = add_low(live.vecs, live.pull.vec_got)
        live.p0 = open_plane(live.pull.d_w_qkv, vecs=live.vecs)
        live = fence(live)

        live.vecs = add_low(live.vecs, live.p0.core.got[-16:])
        first_send(live.p0, live.vecs)
        live.middle = middle
        live.d_inputs = live.d_hidden + dot_nn(live.d_projected, w_qkv)
        del live.d_projected
        live = fence(live)

        live.vecs = add_low(live.vecs, live.p0.upper.got[-16:])
        second_send(live.p0, live.vecs)
        second_send(live.p3)
        first, second = live.middle[:share], live.middle[share:]
        live.inner = jnp.where(odd, first, second)
        live.inner_got = swap(jnp.where(odd, second, first), "z", 4, 1)
        del live.middle
        away = far(live.d_inputs[span:].astype(BF16))
        live = fence(live)

        live.vecs = add_low(live.vecs, live.p0.upper.got[-16:])
        lowest, closed = close(live.pull.p0), close(live.pull.p3)
        live.outer = jnp.where(odd, closed, lowest)
        sent = jnp.where(odd, lowest, closed)
        live.outer_got = swap(jnp.concatenate([sent, live.vecs]), "z", 4, 1)
        live.inner = add_low(live.inner, live.pull.inner_got)
        live.inner_got = lax.ppermute(live.inner, "z", [(3, 1), (0, 2)])
        result_far = far(live.result[span:])
        live = fence(live)

        live.vecs = add_low(live.vecs, live.outer_got[share:])
        live.outer = add_low(live.outer, live.pull.outer_got[:share])
        live.outer_got = lax.ppermute(live.outer, "z", [(2, 0), (1, 3)])
        input_grad = ungroup(live.d_inputs[:span], away.astype(F32))
        block_out = ungroup(live.result[:span], result_far)
        owner = ((z_place * ny + y_place) * nx + x_place) * nc + core
        vecs = live.vecs.astype(F32).reshape(-1)
        own_vecs = lax.dynamic_slice(vecs, (owner * share,), (share,))
        live.inner = live.inner.astype(F32) + live.pull.inner_got.astype(F32)
        live = fence(live)

        outer = live.outer.astype(F32) + live.outer_got.astype(F32)
        own_mats = jnp.where((z_place == 0) | (z_place == 3), outer, live.inner)
    else:
        block_out = ungroup(result[:span], far(result[span:]))
        d_hidden, d_branch, d_mixed, d_b_out, d_gain_one, d_shift_one = hidden_back(
            d_inner, d_hidden_two
        )
        d_w_out = rows_of(d_branch, mixed)

        def send_back(mine, others):
            offset = half // 2
            while offset >= 1:
                rows = offset * nc * count
                got = swap(others[rows - count :], "x", nx, offset)
                mine = add_low(mine, got[:count])
                others = add_low(others[: rows - count], got[count:])
                offset //= 2
            return add_low(mine, swap(others, "core", nc, 1))

        columns = [[], [], []]
        for part in range(2):
            d_query, d_key_own, d_value_own, d_key_other, d_value_other = attend_back(
                part, d_mixed
            )
            columns[0].append(d_query)
            columns[1].append(send_back(d_key_own, d_key_other))
            columns[2].append(send_back(d_value_own, d_value_other))
        d_query, _, d_value = (jnp.concatenate(c, axis=1) for c in columns)
        d_projected = jnp.concatenate([part for c in columns for part in c], axis=1)
        d_w_qkv = rows_of(d_projected, inputs)
        d_inputs = d_hidden + dot_nn(d_projected, w_qkv)
        d_away = far(d_inputs[span:].astype(BF16)).astype(F32)
        input_grad = ungroup(d_inputs[:span], d_away)
        grad_rows = jnp.concatenate([d_w_qkv, d_w_out, d_w_first, d_second_low, d_second_high])
        own_mats = lax.psum_scatter(grad_rows, every, scatter_dimension=0, tiled=True)
        own_mats = own_mats.astype(F32)
        grad_vecs = jnp.concatenate(
            [
                jnp.sum(d_query.astype(F32), axis=0),
                jnp.sum(d_value.astype(F32), axis=0),
                d_b_out,
                d_gain_one,
                d_shift_one,
                d_gain_two,
                d_shift_two,
                d_b_second,
                d_b_first,
            ]
        )
        own_vecs = lax.psum_scatter(grad_vecs, every, scatter_dimension=0, tiled=True)

    new_mats, first_mats, later_mats = adamw(
        mats, own_mats.T, moment_mats, second_mats, rate_mats, weight_decay
    )
    new_vecs, first_vecs, later_vecs = adamw(
        vectors, own_vecs, moment_vecs, second_vecs, rate_vecs, 0.0
    )
    return (
        block_out,
        input_grad,
        new_mats,
        first_mats,
        later_mats,
        new_vecs,
        first_vecs,
        later_vecs,
    )


def solution(mesh):
    dp, seq = mesh.shape["dp"], mesh.shape["seq"]
    ny = 2 ** ((dp.bit_length() - 1) // 2)
    sizes = (dp // ny, ny, seq // 2, 2)
    fine = Mesh(mesh.devices.reshape(sizes), ("z", "y", "x", "core"))
    rows, every = ("z", "y"), ("z", "y", "x", "core")
    tokens = P(rows, ("x", "core"), None)
    return jax.shard_map(
        functools.partial(local, sizes),
        mesh=fine,
        in_specs=(
            tokens,
            P(rows, None),
            tokens,
            P(None, every),
            P(every),
            P(None, every),
            P(None, every),
            P(every),
            P(every),
        ),
        out_specs=(
            tokens,
            tokens,
            P(None, every),
            P(None, every),
            P(None, every),
            P(every),
            P(every),
            P(every),
        ),
        check_vma=False,
    )
```
